512 devices in a mesh: gx: 4 (over z_hi, core), gy: 16 (over y, x), gz: 8 (over z_lo).
Axes of the slice: x: 4, y: 4, z: 16 (z_hi: 2, z_lo: 8; z = z_hi * 8 + z_lo), core: 2. Of those that a mesh axis runs over, the one named last changes fastest.
Arguments:
- positions: float32 [3, 4, 16, 8, 128], P(None, 'gx', 'gy', 'gz'), may hold values from 0 to 10
- species: int32 [4, 16, 8, 128], P('gx', 'gy', 'gz'), may hold values from -1 to 4, as said below
- neighbours: int32 [12, 4, 16, 8, 128], P(None, 'gx', 'gy', 'gz'), may hold values from 99 to 3353, as said below
- embedding: float32 [5, 128], replicated, may hold values from -6 to 6
- basis_first: bfloat16 [8, 64], replicated, may hold values from -2 to 2
- radial_first: bfloat16 [64, 384], replicated, may hold values from -3 to 3
- mixing_first: bfloat16 [384, 128], replicated, may hold values from -1.25 to 1.25
- readout_first: float32 [128], replicated, may hold values from -0.125 to 0.125
- basis_second: bfloat16 [8, 64], replicated, may hold values from -2 to 2
- radial_second: bfloat16 [64, 384], replicated, may hold values from -3 to 3
- mixing_second: bfloat16 [384, 128], replicated, may hold values from -0.3125 to 0.3125
- readout_second: float32 [128], replicated, may hold values from -0.5 to 0.5
- channel_update: bfloat16 [128, 128], replicated, may hold values from -0.5 to 0.5
Outputs:
- energies: float32 [4, 16, 8, 128], P('gx', 'gy', 'gz')
- forces: float32 [3, 4, 16, 8, 128], P(None, 'gx', 'gy', 'gz')
The draws below stay inside these ranges and needn't reach their ends.
Inputs may be any that keep to these rules, and one draw needn't show every extreme that they name: `species`: slots 128 - 3 and above are always empty. `neighbours`: slot t < 125 is sub-cell (t // 25, t // 5 % 5, t % 5) of a 5 x 5 x 5 grid of its cell; an entry code * 128 + t names slot t of the cell at offset (code // 9 - 1, code // 3 % 3 - 1, code % 3 - 1), periodic; t < 125, each entry lies within two sub-cells of the atom's sub-cell (that of slot % 125) along every dimension, never the atom itself; entries may name empty slots.
All inputs are finite; a program needn't handle non-finite values.
Results may differ from the reference program's by a relative error of at most 0.022.
Values may be sent and summed in bfloat16 or wider, within the bound.
A program may use at most 64 MiB of HBM per device.

```python
import math
import jax
import jax.numpy as jnp
import numpy as np
from jax import lax

CHAN = 128
NSPEC = 5
NRAD = 8
RHID = 64
NEIGH = 12
PLACES_PER_BOX = 128
BOXES_ALONG_X = 4
BOXES_ALONG_Y = 16
BOXES_ALONG_Z = 8


adjacent_shift_list = np.array([[first_step, second_step, third_step] for first_step in range(-2, 3) for second_step in range(-2, 3) for third_step in range(-2, 3) if 0 < first_step * first_step + second_step * second_step + third_step * third_step <= 6], dtype=np.int32)


adjacency_reward = np.array([1 << 28 if tuple(matrix_element) == (2, 1, 1) or tuple(matrix_element) == (-2, -1, -1) else 0 for matrix_element in adjacent_shift_list], dtype=np.int32)


def sub_cells(slot_ids):
    site_ids = slot_ids % 125
    return (site_ids // 25, site_ids // 5 % 5, site_ids % 5)


def draw_positions(key, part):
    key = jax.random.fold_in(key, 7)
    sub_x, sub_y, sub_z = sub_cells(jnp.arange(PLACES_PER_BOX, dtype=jnp.int32))
    centres = jnp.stack([sub_x, sub_y, sub_z]).astype(jnp.float32) * 2.0 + 1.0
    shape = (3, BOXES_ALONG_X, BOXES_ALONG_Y, BOXES_ALONG_Z, PLACES_PER_BOX)
    jitter = jax.random.uniform(key, shape, jnp.float32, -0.45, 0.45)
    return centres[:, None, None, None, :] + jitter


def draw_species(key, part):
    key = jax.random.fold_in(key, 11)
    rate_key, roll_key, pick_key = jax.random.split(key, 3)
    shape = (BOXES_ALONG_X, BOXES_ALONG_Y, BOXES_ALONG_Z, PLACES_PER_BOX)
    vacancy = jax.random.randint(rate_key, (BOXES_ALONG_X, BOXES_ALONG_Y, BOXES_ALONG_Z, 1), 0, 4)
    rolled = jax.random.randint(roll_key, shape, 0, 8)
    picked = jax.random.randint(pick_key, shape, 0, 20)
    element = jnp.where(picked < 10, 0, jnp.where(picked < 15, 1, jnp.where(picked < 17, 2, jnp.where(picked < 19, 3, 4))))
    slot_ids = jnp.arange(PLACES_PER_BOX, dtype=jnp.int32)[None, None, None, :]
    filled = (rolled >= vacancy) & (slot_ids < 125)
    return jnp.where(filled, element, -1).astype(jnp.int32)


def draw_neighbours(key, part):
    key = jax.random.fold_in(key, 13)
    running_number = adjacent_shift_list.shape[0]
    ranking_numbers = jax.random.randint(key, (BOXES_ALONG_X, BOXES_ALONG_Y, BOXES_ALONG_Z, PLACES_PER_BOX, running_number), 0, 1 << 20) * 128 + jnp.arange(running_number, dtype=jnp.int32) + jnp.asarray(adjacency_reward)
    chosen = lax.top_k(ranking_numbers, NEIGH)[1]
    steps = jnp.asarray(adjacent_shift_list)[chosen]
    sub_x, sub_y, sub_z = sub_cells(jnp.arange(PLACES_PER_BOX, dtype=jnp.int32))
    reach_x = sub_x[:, None] + steps[..., 0]
    reach_y = sub_y[:, None] + steps[..., 1]
    reach_z = sub_z[:, None] + steps[..., 2]
    move_x = (reach_x + 5) // 5 - 1
    move_y = (reach_y + 5) // 5 - 1
    move_z = (reach_z + 5) // 5 - 1
    cell_code = (move_x + 1) * 9 + (move_y + 1) * 3 + (move_z + 1)
    target = (reach_x - 5 * move_x) * 25 + (reach_y - 5 * move_y) * 5 + (reach_z - 5 * move_z)
    return jnp.moveaxis(cell_code * PLACES_PER_BOX + target, -1, 0).astype(jnp.int32)


def noise(own_key, dims, scale, most, held_as=jnp.bfloat16):
    return jnp.clip(scale * jax.random.normal(own_key, dims, jnp.float32), -most, most).astype(held_as)


def setup_inputs(seed: int = 0) -> dict:
    seeds = jax.random.split(jax.random.key(seed), 14)
    positions = draw_positions(jax.random.fold_in(seeds[13], 71), 0)
    species = draw_species(jax.random.fold_in(seeds[13], 71), 0)
    neighbours = draw_neighbours(jax.random.fold_in(seeds[13], 71), 0)
    embedding = noise(seeds[3], (NSPEC, CHAN), 1.0, 6.0, jnp.float32)
    basis_first = noise(seeds[4], (NRAD, RHID), NRAD ** -0.5, 2.0)
    radial_first = noise(seeds[5], (RHID, 3 * CHAN), 4 ** -0.5, 3.0)
    mixing_first = noise(seeds[6], (3 * CHAN, CHAN), (3 * CHAN // 16) ** -0.5, 1.25)
    readout_first = noise(seeds[7], (CHAN,), (16 * CHAN) ** -0.5, 0.125, jnp.float32)
    basis_second = noise(seeds[8], (NRAD, RHID), NRAD ** -0.5, 2.0)
    radial_second = noise(seeds[9], (RHID, 3 * CHAN), 4 ** -0.5, 3.0)
    mixing_second = noise(seeds[10], (3 * CHAN, CHAN), (3 * CHAN) ** -0.5, 0.3125)
    readout_second = noise(seeds[11], (CHAN,), CHAN ** -0.5, 0.5, jnp.float32)
    channel_update = noise(seeds[12], (CHAN, CHAN), CHAN ** -0.5, 0.5)
    return {"positions": positions, "species": species, "neighbours": neighbours, "embedding": embedding, "basis_first": basis_first, "radial_first": radial_first, "mixing_first": mixing_first, "readout_first": readout_first, "basis_second": basis_second, "radial_second": radial_second, "mixing_second": mixing_second, "readout_second": readout_second, "channel_update": channel_update}


cell_edge = 10.0
cutoff = 5.0

def harmonics(reduced):
    comp_x = reduced[0]
    comp_y = reduced[1]
    comp_z = reduced[2]
    length = comp_x * comp_x + comp_y * comp_y + comp_z * comp_z
    root_three = math.sqrt(3.0)
    root_fifteen = math.sqrt(15.0)
    root_five = math.sqrt(5.0)
    return jnp.stack([jnp.ones_like(comp_x), root_three * comp_x, root_three * comp_y, root_three * comp_z, root_fifteen * comp_x * comp_y, root_fifteen * comp_y * comp_z, 0.5 * root_five * (3.0 * comp_z * comp_z - length), root_fifteen * comp_x * comp_z, 0.5 * root_fifteen * (comp_x * comp_x - comp_y * comp_y)])

def interact(centre, position_table, live_table, feature_table, index_block, offset_block, radial_in, radial_out, mixing):
    nearby, block_atoms = index_block.shape
    channels = feature_table.shape[1]
    radial_count = radial_in.shape[0]
    flat_index = index_block.reshape(-1)
    displace = jnp.take(position_table, flat_index, axis=1).reshape(3, nearby, block_atoms) + offset_block - centre[:, None, :]
    reduced = (displace / cutoff).reshape(3, nearby * block_atoms)
    squared = lax.optimization_barrier(jnp.sum(reduced * reduced, axis=0))
    envelope = jnp.square(jnp.maximum(1.0 - squared, 0.0)) * jnp.take(live_table, flat_index)
    centers = jnp.arange(radial_count, dtype=jnp.float32) / (radial_count - 1)
    radial_basis = jnp.exp(-jnp.square((squared[:, None] - centers[None, :]) * (radial_count - 1))).astype(jnp.bfloat16)
    hidden = jax.nn.silu(jnp.dot(radial_basis, radial_in, preferred_element_type=jnp.float32)).astype(jnp.bfloat16)
    radial = jnp.dot(hidden, radial_out, preferred_element_type=jnp.float32) * envelope[:, None]
    harmonic_vals = harmonics(reduced).reshape(9, nearby, block_atoms)
    neighbour = jnp.take(feature_table, flat_index, axis=0)
    scaling = 1.0 / math.sqrt(nearby)
    pieces = []
    for degree, (start_row, stop_row) in enumerate(((0, 1), (1, 4), (4, 9))):
        weighted = (radial[:, degree * channels:(degree + 1) * channels] * neighbour).reshape(nearby, block_atoms, channels)
        pieces.append(jnp.einsum('mkb,kbc->bmc', harmonic_vals[start_row:stop_row], weighted) * scaling)
    mixed_in = jnp.concatenate([pieces[0][:, 0, :], lax.optimization_barrier(jnp.sum(pieces[1] * pieces[1], axis=1)), lax.optimization_barrier(jnp.sum(pieces[2] * pieces[2], axis=1))], axis=1).astype(jnp.bfloat16)
    return jax.nn.silu(jnp.dot(mixed_in, mixing, preferred_element_type=jnp.float32))

def run_layer(centres, position_table, live_table, feature_table, index_blocks, offset_blocks, radial_in, radial_out, mixing):
    checked = jax.checkpoint(interact)

    def one_block(pieces):
        return checked(pieces[0], position_table, live_table, feature_table, pieces[1], pieces[2], radial_in, radial_out, mixing)
    result = lax.map(one_block, (centres, index_blocks, offset_blocks))
    return result.reshape(-1, result.shape[-1])

def lookup(species_ids, embedding):
    summed = jnp.zeros(species_ids.shape + (embedding.shape[1],), jnp.float32)
    for element in range(embedding.shape[0]):
        summed = summed + (species_ids == element).astype(jnp.float32)[..., None] * embedding[element][None, :]
    return summed

def decode(neighbours, slots):
    cell_code = neighbours // slots
    target = neighbours % slots
    return (target, cell_code // 9 - 1, cell_code // 3 % 3 - 1, cell_code % 3 - 1)

def reference(positions, species, neighbours, embedding, basis_first, radial_first, mixing_first, readout_first, basis_second, radial_second, mixing_second, readout_second, channel_update):
    grid_x, grid_y, grid_z, slots = species.shape
    nearby = neighbours.shape[0]
    atom_count = grid_x * grid_y * grid_z * slots
    block_atoms = slots
    blocks = atom_count // block_atoms
    target, step_x, step_y, step_z = decode(neighbours, slots)
    cell_x = lax.broadcasted_iota(jnp.int32, neighbours.shape, 1)
    cell_y = lax.broadcasted_iota(jnp.int32, neighbours.shape, 2)
    cell_z = lax.broadcasted_iota(jnp.int32, neighbours.shape, 3)
    global_index = (((cell_x + step_x) % grid_x * grid_y + (cell_y + step_y) % grid_y) * grid_z + (cell_z + step_z) % grid_z) * slots + target
    offset = cell_edge * jnp.stack([step_x, step_y, step_z]).astype(jnp.float32)
    index_blocks = global_index.astype(jnp.int32).reshape(nearby, blocks, block_atoms).transpose(1, 0, 2)
    offset_blocks = offset.reshape(3, nearby, blocks, block_atoms).transpose(2, 0, 1, 3)
    species_flat = species.reshape(-1)
    live_table = (species_flat >= 0).astype(jnp.float32)
    start_table = lookup(species_flat, embedding)

    def total_energy(coords):
        position_table = coords.reshape(3, atom_count)
        centres = position_table.reshape(3, blocks, block_atoms).transpose(1, 0, 2)
        node_one = run_layer(centres, position_table, live_table, start_table, index_blocks, offset_blocks, basis_first, radial_first, mixing_first)
        first_state = node_one + start_table
        energy_one = jnp.dot(first_state, readout_first, precision=lax.Precision.HIGHEST)
        update = jnp.dot(first_state.astype(jnp.bfloat16), channel_update, preferred_element_type=jnp.float32).astype(jnp.bfloat16)
        node_two = run_layer(centres, position_table, live_table, update.astype(jnp.float32), index_blocks, offset_blocks, basis_second, radial_second, mixing_second)
        energy_two = jnp.dot(node_two, readout_second, precision=lax.Precision.HIGHEST)
        energies = live_table * (energy_one + energy_two)
        return (jnp.sum(energies), energies)
    (summed, energies), gradient = jax.value_and_grad(total_energy, has_aux=True)(positions)
    return (energies.reshape(species.shape), -gradient)
```

```python
import functools
import itertools
import math

import jax
import jax.numpy as jnp
import numpy as np
from jax import lax
from jax.experimental import pallas as pl
from jax.experimental.pallas import tpu as pltpu
from jax.sharding import PartitionSpec as P

MESH = pl.DeviceIdType.MESH
F32 = jnp.float32
BF16 = jnp.bfloat16
LANES = 128
CHAN = 128
RHID = 64
NEIGH = 12
CELLS = 27
OWN = 13
BLOCKS = 6
PAIRS = NEIGH * LANES
ROOT3 = math.sqrt(3.0)
ROOT5 = math.sqrt(5.0)
ROOT15 = math.sqrt(15.0)
SCALE = 1.0 / math.sqrt(NEIGH)
DEGREES = ((0, 1), (1, 4), (4, 9))
DIRS = [d for d in itertools.product(range(3), (-1, 0, 1), (-1, 0, 1)) if d != (1, 0, 0)]
DIRS.sort(key=lambda d: (d[0], -abs(d[1]) - abs(d[2])))


def cell_number(f, dy, dz):
    return f * 9 + (dy + 1) * 3 + dz + 1


def site_table():
    sites = []
    depth = {-1: (3, 4), 0: range(5), 1: (0, 1)}
    for f, dy, dz in itertools.product(range(3), (-1, 0, 1), (-1, 0, 1)):
        if (f, dy, dz) == (1, 0, 0):
            continue
        for tx, ty, tz in itertools.product(depth[f - 1], depth[dy], depth[dz]):
            rest = ty * 5 + tz
            needs_far = (f - 1) * 5 + tx + 2 < 4
            sites.append((needs_far, tx * 25 + rest, (4 - tx) * 25 + rest, cell_number(f, dy, dz)))
    sites.sort(key=lambda s: s[0])
    table = np.zeros((BLOCKS, 8, LANES), np.float32)
    table[:, 0:2] = -1.0
    table[:, 2] = OWN
    table[0, 0:2] = np.arange(LANES)
    for n, (_, before, after, cell) in enumerate(sites):
        block, lane = 1 + n // LANES, n % LANES
        table[block, 0:3, lane] = (before, after, cell)
    return table


def dot(a, b):
    return jnp.dot(a, b, preferred_element_type=F32)


def dot_nt(a, b):
    return lax.dot_general(a, b, (((1,), (1,)), ((), ())), preferred_element_type=F32)


def sigmoid(v):
    return 0.5 * jnp.tanh(0.5 * v) + 0.5


def padded_t(value):
    rows, columns = value.shape
    if rows < LANES:
        value = jnp.concatenate([value, jnp.zeros((LANES - rows, columns), F32)], axis=0)
    if columns < LANES:
        value = jnp.concatenate([value, jnp.zeros((LANES, LANES - columns), F32)], axis=1)
    return value.T


def kernel(
    sizes,
    pos_ref, spc_ref, nbr_ref, emb_ref, b1_ref, r1_ref, m1_ref, ro1_ref,
    b2_ref, r2_ref, m2_ref, ro2_ref, cu_ref, con_ref,
    en_ref, fo_ref,
    tiles, tpos, tnb, gsend, grecv,
    cpos, code, slot, tcell, oh, oh_site, pg, gs, geo, yb, rb, rbd, spoh,
    g, feat, ds, a_s, inv, node, dnode, upd, dupd, da, dr, dfe, gacc, prt, q, ml, sc,
    win, wout, mix, cut, embt, winp, rocol,
    send_a, recv_a, send_d, recv_d,
):
    nx, ny, nz = sizes
    gx, gy, gz = lax.axis_index("gx"), lax.axis_index("gy"), lax.axis_index("gz")
    sigma = 1 - 2 * lax.rem(gx, 2)

    def device(f, dy, dz):
        return (
            lax.rem(gx + (f - 1) * sigma + nx, nx),
            lax.rem(gy + dy + ny, ny),
            lax.rem(gz + dz + nz, nz),
        )

    barrier = pltpu.get_barrier_semaphore()
    for d in DIRS:
        pl.semaphore_signal(barrier, inc=1, device_id=device(*d), device_id_type=MESH)

    for m in range(3):
        tiles[OWN, m : m + 1, :] = pos_ref[m, 0, 0]
    tiles[OWN, 3:4, :] = spc_ref[0, 0].astype(F32)
    for k in range(NEIGH):
        tiles[OWN, 4 + k : 5 + k, :] = nbr_ref[k, 0, 0].astype(F32)

    for layer, (b_ref, r_ref, m_ref) in enumerate(((b1_ref, r1_ref, m1_ref), (b2_ref, r2_ref, m2_ref))):
        basis = b_ref[...].astype(F32)
        win[layer] = padded_t(basis)[0:RHID, 0:16].astype(BF16)
        winp[layer] = jnp.concatenate([basis, jnp.zeros_like(basis)], axis=0).astype(BF16)
        for l in range(3):
            block = r_ref[:, l * CHAN : (l + 1) * CHAN].astype(F32)
            wout[layer, l * CHAN : (l + 1) * CHAN, :] = padded_t(block)[:, 0:RHID].astype(BF16)
            block = m_ref[l * CHAN : (l + 1) * CHAN, :].astype(F32)
            mix[layer, :, l * CHAN : (l + 1) * CHAN] = block.T.astype(BF16)
    cut[...] = cu_ref[...].astype(F32).T.astype(BF16)
    emb = jnp.concatenate([emb_ref[...], jnp.zeros((3, CHAN), F32)], axis=0)
    emb_hi = emb.astype(BF16).astype(F32)
    both = jnp.concatenate([emb_hi, emb - emb_hi], axis=0)
    embt[...] = padded_t(both)[:, 0:16].astype(BF16)
    for layer, ro_ref in enumerate((ro1_ref, ro2_ref)):
        rocol[layer] = jnp.broadcast_to(ro_ref[...].reshape(1, CHAN), (LANES, CHAN)).T

    pl.semaphore_wait(barrier, len(DIRS))
    copies = []
    for n, (f, dy, dz) in enumerate(DIRS):
        copy = pltpu.make_async_remote_copy(
            src_ref=tiles.at[OWN],
            dst_ref=tiles.at[cell_number(f, -dy, -dz)],
            send_sem=send_a.at[n],
            recv_sem=recv_a.at[n],
            device_id=device(f, dy, dz),
            device_id_type=MESH,
        )
        copy.start()
        copies.append(copy)
    for copy in copies:
        copy.wait_recv()

    sigma_f = sigma.astype(F32)
    row8 = lax.broadcasted_iota(jnp.int32, (8, LANES), 0)
    row16 = lax.broadcasted_iota(jnp.int32, (16, LANES), 0)
    rowf = lax.broadcasted_iota(jnp.int32, (LANES, LANES), 0).astype(F32)
    spec16 = jnp.where(row16 < 8, row16, row16 - 8).astype(F32)
    basis_centre = row8.astype(F32) * (1.0 / 7.0)

    @pl.loop(0, CELLS)
    def _(c):
        top = tiles[c, 0:8, :]
        high = top.astype(BF16).astype(F32)
        low = pltpu.roll(top - high, 4, 0)
        pg[pl.ds(pl.multiple_of(c * 8, 8), 8), 0:LANES] = jnp.where(row8 < 4, high, low)
        entries = tiles[c, 4:16, :]
        codes = jnp.floor((entries + 0.5) * (1.0 / LANES))
        start = pl.multiple_of(c * 24, 8)
        prt[pl.ds(start, 24), :] = jnp.concatenate([codes, entries - LANES * codes], axis=0)

    tpos[0 : CELLS * 8, :] = pg[0 : CELLS * 8, 0:LANES].astype(BF16)
    tpos[CELLS * 8 :, :] = jnp.zeros((8, LANES), BF16)
    tnb[...] = prt[0 : CELLS * 24, :].astype(BF16)

    own_top = tiles[OWN, 0:8, :]
    cpos[0] = own_top
    code[0] = prt[OWN * 24 : OWN * 24 + 12, :]
    slot[0] = prt[OWN * 24 + 12 : OWN * 24 + 24, :]

    def lane_slot(j):
        rows = con_ref[j]
        return jnp.where(sigma_f > 0, rows[0:1], rows[1:2]), rows[2:3]

    for j in range(BLOCKS):
        own_slot, own_cell = lane_slot(j)
        oh[j, :, PAIRS:] = (rowf == own_slot).astype(BF16)
        ident = own_cell * LANES + own_slot
        ident = jnp.where(own_slot < 0, -1.0, ident)
        column = jnp.broadcast_to(ident, (LANES, LANES)).T
        node[j] = column

    @pl.loop(1, BLOCKS)
    def _(j):
        rows = con_ref[j]
        cell = jnp.broadcast_to(rows[2:3], (8, LANES))
        hot = oh[j, :, PAIRS:]
        pg[0 : CELLS * 8 + 8, 0:LANES] = dot(tpos[...], hot)
        prt[0 : CELLS * 24, :] = dot(tnb[...], hot)
        acc = [jnp.zeros((8, LANES), F32) for _ in range(4)]
        for c in range(CELLS):
            here = cell == float(c)
            acc[0] = jnp.where(here, pg[c * 8 : c * 8 + 8, 0:LANES], acc[0])
            for part in range(3):
                rows_at = c * 24 + part * 8
                acc[1 + part] = jnp.where(here, prt[rows_at : rows_at + 8, :], acc[1 + part])
        cpos[j] = acc[0] + pltpu.roll(acc[0], 4, 0)
        both = jnp.concatenate(acc[1:], axis=0)
        code[j] = both[0:12]
        slot[j] = both[12:24]

    @pl.loop(0, BLOCKS)
    def _(j):
        rows = con_ref[j]
        codes, slots = code[j], slot[j]
        nine = jnp.floor((codes + 0.5) * (1.0 / 9.0))
        three = jnp.floor((codes + 0.5) * (1.0 / 3.0))
        step_x = nine - 1.0
        step_y = three - 3.0 * nine - 1.0
        step_z = codes - 3.0 * three - 1.0
        target = rows[2:3] + 9.0 * sigma_f * step_x + 3.0 * step_y + step_z
        tcell[j, 0:12] = target
        tcell[j, 12:13] = rows[2:3]
        for k in range(NEIGH):
            oh[j, :, k * LANES : (k + 1) * LANES] = (rowf == slots[k : k + 1]).astype(BF16)
        for h in range(PAIRS // 256):
            lanes = slice(h * 256, (h + 1) * 256)
            pg[:, lanes] = dot(tpos[...], oh[j, :, lanes])
        for k in range(NEIGH):
            lanes = slice(k * LANES, (k + 1) * LANES)
            here = jnp.broadcast_to(target[k : k + 1], (8, LANES))
            acc = jnp.zeros((8, LANES), F32)
            for c in range(CELLS):
                acc = jnp.where(here == float(c), pg[c * 8 : c * 8 + 8, lanes], acc)
            gs[k * 8 : (k + 1) * 8, :] = acc + pltpu.roll(acc, 4, 0)
        centre = cpos[j]
        x = (gs[pl.ds(0, 12, stride=8), :] + 10.0 * step_x - centre[0:1]) / 5.0
        y = (gs[pl.ds(1, 12, stride=8), :] + 10.0 * step_y - centre[1:2]) / 5.0
        z = (gs[pl.ds(2, 12, stride=8), :] + 10.0 * step_z - centre[2:3]) / 5.0
        species = gs[pl.ds(3, 12, stride=8), :]
        s = x * x + y * y + z * z
        inside = jnp.maximum(1.0 - s, 0.0)
        alive = inside * (species > -0.5).astype(F32)
        env = inside * alive
        geo[j, 0] = x
        geo[j, 1] = y
        geo[j, 2] = z
        geo[j, 3] = env
        geo[j, 4] = alive
        harm = [
            env,
            env * (ROOT3 * x),
            env * (ROOT3 * y),
            env * (ROOT3 * z),
            env * (ROOT15 * x * y),
            env * (ROOT15 * y * z),
            env * (0.5 * ROOT5 * (3.0 * z * z - s)),
            env * (ROOT15 * x * z),
            env * (0.5 * ROOT15 * (x * x - y * y)),
        ]
        for k in range(NEIGH):
            lanes = slice(k * LANES, (k + 1) * LANES)
            for m in range(9):
                yb[j, k, m] = jnp.broadcast_to(harm[m][k : k + 1], (8, LANES))
            t = (jnp.broadcast_to(s[k : k + 1], (8, LANES)) - basis_centre) * 7.0
            e = jnp.exp(-(t * t))
            rb[j, :, lanes] = jnp.concatenate([e, e], axis=0).astype(BF16)
            rbd[j, :, lanes] = e * (-14.0 * t)
            spoh[j, :, lanes] = (spec16 == species[k : k + 1]).astype(BF16)

    def radial(layer, j, at):
        for h in range(PAIRS // 256):
            lanes = slice(h * 256, (h + 1) * 256)
            pre = dot(win[layer], rb[j, :, lanes])
            sig = sigmoid(pre)
            hid = pre * sig
            ds[at, :, lanes] = sig + hid * (1.0 - sig)
            out = dot(wout[layer], hid.astype(BF16))
            g[at, 2 * h] = out[:, 0:LANES]
            g[at, 2 * h + 1] = out[:, LANES:]

    def gather_sum(j, at, second):
        @pl.loop(0, CHAN // 8)
        def _(ct):
            start = pl.multiple_of(ct * 8, 8)
            acc = [None] * 9
            for k in range(NEIGH):
                f = feat[at, k, pl.ds(start, 8), :]
                for l, (low, high) in enumerate(DEGREES):
                    here = pl.ds(pl.multiple_of(l * CHAN + start, 8), 8)
                    value = g[at, k, here, :] * f
                    if not second:
                        g[at, k, here, :] = value
                    for m in range(low, high):
                        term = value * yb[j, k, m]
                        acc[m] = term if k == 0 else acc[m] + term
            acc = [a * SCALE for a in acc]
            for m in range(9):
                a_s[at, m, pl.ds(start, 8), :] = acc[m]
            one = acc[1] * acc[1] + acc[2] * acc[2] + acc[3] * acc[3]
            two = acc[4] * acc[4] + acc[5] * acc[5] + acc[6] * acc[6] + acc[7] * acc[7] + acc[8] * acc[8]
            for l, value in enumerate((acc[0], one, two)):
                inv[pl.ds(pl.multiple_of(l * CHAN + start, 8), 8), :] = value

    def sums_back(layer, at, dpre):
        dinv = dot(mix_refs[layer][...], dpre.astype(BF16))
        da[0] = SCALE * dinv[0:CHAN]
        for l, (low, high) in enumerate(DEGREES[1:], 1):
            part = (2.0 * SCALE) * dinv[l * CHAN : (l + 1) * CHAN]
            for m in range(low, high):
                da[m] = a_s[at, m] * part

    def pair_back(layer, j, at, second):
        @pl.loop(0, NEIGH // 2)
        def _(h):
            for half in range(2):
                k = 2 * h + half
                harm = [yb[j, k, m] for m in range(9)]
                sums = [None] * 9
                for ct in range(CHAN // 8):
                    chans = slice(ct * 8, ct * 8 + 8)
                    f = feat[at, k, chans, :]
                    cots = [da[m, chans, :] for m in range(9)]
                    df = None
                    for l, (low, high) in enumerate(DEGREES):
                        rows = slice(l * CHAN + ct * 8, l * CHAN + ct * 8 + 8)
                        r = g[at, k, rows, :]
                        value = r * f if second else r
                        dval = None
                        for m in range(low, high):
                            part = cots[m] * value
                            sums[m] = part if ct == 0 else sums[m] + part
                            part = cots[m] * harm[m]
                            dval = part if dval is None else dval + part
                        dr[rows, half * LANES : (half + 1) * LANES] = dval * f
                        if second:
                            df = dval * r if df is None else df + dval * r
                    if second:
                        dfe[chans, pl.ds(pl.multiple_of(k * LANES, LANES), LANES)] = df
                for m in range(9):
                    prt[pl.ds(pl.multiple_of(m * 96 + k * 8, 8), 8), :] = sums[m]
            lanes = pl.ds(pl.multiple_of(h * 256, 256), 256)
            dhid = dot(radial_refs[layer][...], dr[...].astype(BF16))
            dpre = (dhid * ds[at, :, lanes]).astype(BF16)
            drb = dot(winp[layer], dpre)[0:8] * rbd[j, :, lanes]
            q[pl.ds(pl.multiple_of(h * 16, 8), 8), :] = drb[:, 0:LANES]
            q[pl.ds(pl.multiple_of(h * 16 + 8, 8), 8), :] = drb[:, LANES:]

    def eight(ref, base):
        total = ref[pl.ds(base, 12, stride=8), :]
        for r in range(1, 8):
            total = total + ref[pl.ds(base + r, 12, stride=8), :]
        return total

    def geometry_back(j):
        x, y, z, env, alive = (geo[j, n] for n in range(5))
        s = x * x + y * y + z * z
        d = [eight(prt, m * 96) for m in range(9)]
        harm = [
            None,
            ROOT3 * x,
            ROOT3 * y,
            ROOT3 * z,
            ROOT15 * x * y,
            ROOT15 * y * z,
            0.5 * ROOT5 * (3.0 * z * z - s),
            ROOT15 * x * z,
            0.5 * ROOT15 * (x * x - y * y),
        ]
        denv = d[0]
        for m in range(1, 9):
            denv = denv + d[m] * harm[m]
        dsq = eight(q, 0) - 2.0 * denv * alive
        d = [None] + [env * value for value in d[1:]]
        d6 = ROOT5 * d[6]
        dx = 2.0 * x * dsq + ROOT3 * d[1] + ROOT15 * (y * d[4] + z * d[7] + x * d[8]) - x * d6
        dy = 2.0 * y * dsq + ROOT3 * d[2] + ROOT15 * (x * d[4] + z * d[5] - y * d[8]) - y * d6
        dz = 2.0 * z * dsq + ROOT3 * d[3] + ROOT15 * (y * d[5] + x * d[7]) + 2.0 * z * d6
        return dx, dy, dz

    radial_refs = (r1_ref, r2_ref)
    mix_refs = (m1_ref, m2_ref)

    for k in range(NEIGH):
        lanes = slice(k * LANES, (k + 1) * LANES)
        ident = tcell[0, k : k + 1, :] * LANES + slot[0, k : k + 1, :]
        for j in range(BLOCKS):
            oh_site[j * LANES : (j + 1) * LANES, lanes] = (node[j] == ident).astype(BF16)

    @pl.loop(0, BLOCKS)
    def _(j):
        for h in range(PAIRS // 256):
            out = dot(embt[...], spoh[j, :, h * 256 : (h + 1) * 256])
            feat[j, 2 * h] = out[:, 0:LANES]
            feat[j, 2 * h + 1] = out[:, LANES:]
        radial(0, j, j)
        gather_sum(j, j, False)
        pre = dot(mix[0], inv[...].astype(BF16))
        sig = sigmoid(pre)
        value = pre * sig
        dnode[j] = sig + value * (1.0 - sig)
        hot = (spec16 == cpos[j, 3:4, :]).astype(BF16)
        state = value + dot(embt[...], hot)
        node[j] = state
        upd[:, pl.ds(pl.multiple_of(j * LANES, LANES), LANES)] = dot(cut[...], state.astype(BF16)).astype(BF16)

    radial(1, 0, BLOCKS)
    for h in range(PAIRS // 256):
        out = dot(upd[...], oh_site[:, h * 256 : (h + 1) * 256])
        feat[BLOCKS, 2 * h] = out[:, 0:LANES]
        feat[BLOCKS, 2 * h + 1] = out[:, LANES:]
    gather_sum(0, BLOCKS, True)
    live = (cpos[0, 3:4, :] > -0.5).astype(F32)
    pre = dot(mix[1], inv[...].astype(BF16))
    sig = sigmoid(pre)
    value = pre * sig
    energy = jnp.sum(rocol[0] * node[0] + rocol[1] * value, axis=0, keepdims=True)
    en_ref[0, 0] = live * energy

    sums_back(1, BLOCKS, rocol[1] * live * (sig + value * (1.0 - sig)))
    pair_back(1, 0, BLOCKS, True)
    for m, value in enumerate(geometry_back(0)):
        gacc[0, m] = value
    gacc[1:] = jnp.zeros((BLOCKS - 1, 3, NEIGH, LANES), F32)
    for h in range(BLOCKS // 2):
        rows = slice(h * 256, (h + 1) * 256)
        dupd[:, rows] = dot_nt(dfe[...].astype(BF16), oh_site[rows, :]).astype(BF16)
    for j in range(BLOCKS):
        back = dot(cu_ref[...], dupd[:, j * LANES : (j + 1) * LANES])
        if j == 0:
            back = back + rocol[0] * live
        node[j] = back

    sc[...] = jnp.zeros_like(sc)

    @pl.loop(0, BLOCKS)
    def _(j):
        sums_back(0, j, node[j] * dnode[j])
        pair_back(0, j, j, False)
        parts = []
        for m, value in enumerate(geometry_back(j)):
            value = (value + gacc[j, m]) * 0.2
            whole = jnp.concatenate([value, -jnp.sum(value, axis=0, keepdims=True)], axis=0)
            high = whole.astype(BF16).astype(F32)
            parts.append((high, whole - high))
        for k in range(NEIGH + 1):
            tile = jnp.zeros((8, LANES), F32)
            for m in range(3):
                for n in range(2):
                    tile = jnp.where(row8 == m + 4 * n, parts[m][n][k : k + 1], tile)
            where = jnp.broadcast_to(tcell[j, k : k + 1, :], (8, LANES))
            lanes = slice(k * LANES, (k + 1) * LANES)
            for c in range(0, CELLS + 1, 2):
                pair = [jnp.where(where == float(c + n), tile, 0.0) for n in range(2)]
                ml[c * 8 : c * 8 + 16, lanes] = jnp.concatenate(pair, axis=0).astype(BF16)
        sc[...] += dot_nt(ml[...], oh[j])

    @pl.loop(0, CELLS)
    def _(c):
        rows = sc[pl.ds(pl.multiple_of(c * 8, 8), 8), :]
        gsend[c] = rows + pltpu.roll(rows, 4, 0)

    returns = []
    for n, (f, dy, dz) in enumerate(DIRS):
        copy = pltpu.make_async_remote_copy(
            src_ref=gsend.at[cell_number(f, dy, dz)],
            dst_ref=grecv.at[cell_number(f, -dy, -dz)],
            send_sem=send_d.at[n],
            recv_sem=recv_d.at[n],
            device_id=device(f, dy, dz),
            device_id_type=MESH,
        )
        copy.start()
        returns.append(copy)
    for copy in copies:
        copy.wait_send()
    for copy in returns:
        copy.wait_recv()
    total = gsend[OWN]
    for d in DIRS:
        total = total + grecv[cell_number(*d)]
    for m in range(3):
        fo_ref[m, 0, 0] = -total[m : m + 1]
    for copy in returns:
        copy.wait_send()


def body(sizes, positions, species, neighbours, *weights):
    table = jnp.asarray(site_table())
    vmem = pl.BlockSpec(memory_space=pltpu.VMEM)
    n = len(DIRS)
    scratch = [
        pltpu.VMEM((CELLS, 16, LANES), F32),
        pltpu.VMEM((CELLS * 8 + 8, LANES), BF16),
        pltpu.VMEM((CELLS * 24, LANES), BF16),
        pltpu.VMEM((CELLS, 8, LANES), F32),
        pltpu.VMEM((CELLS, 8, LANES), F32),
        pltpu.VMEM((BLOCKS, 8, LANES), F32),
        pltpu.VMEM((BLOCKS, NEIGH, LANES), F32),
        pltpu.VMEM((BLOCKS, NEIGH, LANES), F32),
        pltpu.VMEM((BLOCKS, 16, LANES), F32),
        pltpu.VMEM((BLOCKS, LANES, PAIRS + LANES), BF16),
        pltpu.VMEM((BLOCKS * LANES, PAIRS), BF16),
        pltpu.VMEM((CELLS * 8 + 8, PAIRS), F32),
        pltpu.VMEM((96, LANES), F32),
        pltpu.VMEM((BLOCKS, 5, NEIGH, LANES), F32),
        pltpu.VMEM((BLOCKS, NEIGH, 9, 8, LANES), F32),
        pltpu.VMEM((BLOCKS, 16, PAIRS), BF16),
        pltpu.VMEM((BLOCKS, 8, PAIRS), F32),
        pltpu.VMEM((BLOCKS, 16, PAIRS), BF16),
        pltpu.VMEM((BLOCKS + 1, NEIGH, 3 * CHAN, LANES), F32),
        pltpu.VMEM((BLOCKS + 1, NEIGH, CHAN, LANES), F32),
        pltpu.VMEM((BLOCKS + 1, RHID, PAIRS), F32),
        pltpu.VMEM((BLOCKS + 1, 9, CHAN, LANES), F32),
        pltpu.VMEM((3 * CHAN, LANES), F32),
        pltpu.VMEM((BLOCKS, CHAN, LANES), F32),
        pltpu.VMEM((BLOCKS, CHAN, LANES), F32),
        pltpu.VMEM((CHAN, BLOCKS * LANES), BF16),
        pltpu.VMEM((CHAN, BLOCKS * LANES), BF16),
        pltpu.VMEM((9, CHAN, LANES), F32),
        pltpu.VMEM((3 * CHAN, 2 * LANES), F32),
        pltpu.VMEM((CHAN, PAIRS), F32),
        pltpu.VMEM((BLOCKS, 3, NEIGH, LANES), F32),
        pltpu.VMEM((9 * 96, LANES), F32),
        pltpu.VMEM((96, LANES), F32),
        pltpu.VMEM((CELLS * 8 + 8, PAIRS + LANES), BF16),
        pltpu.VMEM((CELLS * 8 + 8, LANES), F32),
        pltpu.VMEM((2, RHID, 16), BF16),
        pltpu.VMEM((2, 3 * CHAN, RHID), BF16),
        pltpu.VMEM((2, CHAN, 3 * CHAN), BF16),
        pltpu.VMEM((CHAN, CHAN), BF16),
        pltpu.VMEM((CHAN, 16), BF16),
        pltpu.VMEM((2, 16, RHID), BF16),
        pltpu.VMEM((2, CHAN, LANES), F32),
    ] + [pltpu.SemaphoreType.DMA((n,))] * 4
    return pl.pallas_call(
        functools.partial(kernel, sizes),
        out_shape=(
            jax.ShapeDtypeStruct(species.shape, F32),
            jax.ShapeDtypeStruct(positions.shape, F32),
        ),
        in_specs=[vmem] * 14,
        out_specs=(vmem, vmem),
        scratch_shapes=scratch,
        compiler_params=pltpu.CompilerParams(
            collective_id=0, has_side_effects=True, vmem_limit_bytes=56 << 20
        ),
    )(positions, species, neighbours, *weights, table)


def solution(mesh):
    sizes = tuple(mesh.shape[axis] for axis in ("gx", "gy", "gz"))
    grid = ("gx", "gy", "gz", None)
    return jax.shard_map(
        functools.partial(body, sizes),
        mesh=mesh,
        in_specs=(P(None, *grid), P(*grid), P(None, *grid)) + (P(),) * 10,
        out_specs=(P(*grid), P(None, *grid)),
        check_vma=False,
    )
```

```python
import functools
import itertools
import math

import jax
import jax.numpy as jnp
import numpy as np
from jax import lax
from jax.experimental import pallas as pl
from jax.experimental.pallas import tpu as pltpu
from jax.sharding import PartitionSpec as P

MESH = pl.DeviceIdType.MESH
F32 = jnp.float32
BF16 = jnp.bfloat16
LANES = 128
CHAN = 128
RHID = 64
NEIGH = 12
CELLS = 27
OWN = 13
BLOCKS = 6
FAR_BLOCKS = 4
PAIRS = NEIGH * LANES
ROOT3 = math.sqrt(3.0)
ROOT5 = math.sqrt(5.0)
ROOT15 = math.sqrt(15.0)
SCALE = 1.0 / math.sqrt(NEIGH)
DEGREES = ((0, 1), (1, 4), (4, 9))
DIRS = [d for d in itertools.product(range(3), (-1, 0, 1), (-1, 0, 1)) if d != (1, 0, 0)]
DIRS.sort(key=lambda d: (d[0], -abs(d[1]) - abs(d[2])))


def cell_number(f, dy, dz):
    return f * 9 + (dy + 1) * 3 + dz + 1


def site_table():
    sites = []
    depth = {-1: (3, 4), 0: range(5), 1: (0, 1)}
    for f, dy, dz in itertools.product(range(3), (-1, 0, 1), (-1, 0, 1)):
        if (f, dy, dz) == (1, 0, 0):
            continue
        for tx, ty, tz in itertools.product(depth[f - 1], depth[dy], depth[dz]):
            rest = ty * 5 + tz
            sites.append(((f - 1) * 5 + tx, tx * 25 + rest, (4 - tx) * 25 + rest, cell_number(f, dy, dz)))
    sites.sort(key=lambda s: -s[0])
    near = (BLOCKS - FAR_BLOCKS) * LANES
    sites = sites[near:][::-1] + [None] * (BLOCKS * LANES - LANES - len(sites)) + sites[:near]
    table = np.zeros((BLOCKS, 8, LANES), np.float32)
    table[:, 0:2] = -1.0
    table[:, 2] = OWN
    table[0, 0:2] = np.arange(LANES)
    for n, site in enumerate(sites):
        if site is not None:
            table[1 + n // LANES, 0:3, n % LANES] = site[1:]
    return table


def dot(a, b):
    return jnp.dot(a, b, preferred_element_type=F32)


def dot_nt(a, b):
    return lax.dot_general(a, b, (((1,), (1,)), ((), ())), preferred_element_type=F32)


def sigmoid(v):
    return 0.5 * jnp.tanh(0.5 * v) + 0.5


def padded_t(value):
    rows, columns = value.shape
    if rows < LANES:
        value = jnp.concatenate([value, jnp.zeros((LANES - rows, columns), F32)], axis=0)
    if columns < LANES:
        value = jnp.concatenate([value, jnp.zeros((LANES, LANES - columns), F32)], axis=1)
    return value.T


def kernel(
    sizes,
    pos_ref, spc_ref, nbr_ref, emb_ref, b1_ref, r1_ref, m1_ref, ro1_ref,
    b2_ref, r2_ref, m2_ref, ro2_ref, cu_ref, con_ref,
    en_ref, fo_ref,
    tiles, tpos, tnb, gsend, grecv,
    cpos, code, slot, tcell, oh, oh_site, pg, gs, column, geo, yb, rb, rbd, spoh,
    g, feat, ds, a_s, inv, node, dnode, upd, dupd, da, dr, dfe, gacc, prt, q, ml, sc, dpr,
    win, wout, mix, cut, embt, winp, rocol,
    send_a, recv_a, send_d, recv_d,
):
    nx, ny, nz = sizes
    gx, gy, gz = lax.axis_index("gx"), lax.axis_index("gy"), lax.axis_index("gz")
    sigma = 1 - 2 * lax.rem(gx, 2)

    def device(f, dy, dz):
        return (
            lax.rem(gx + (f - 1) * sigma + nx, nx),
            lax.rem(gy + dy + ny, ny),
            lax.rem(gz + dz + nz, nz),
        )

    barrier = pltpu.get_barrier_semaphore()
    for d in DIRS:
        pl.semaphore_signal(barrier, inc=1, device_id=device(*d), device_id_type=MESH)

    for m in range(3):
        tiles[OWN, m : m + 1, :] = pos_ref[m, 0, 0]
    tiles[OWN, 3:4, :] = spc_ref[0, 0].astype(F32)
    for k in range(NEIGH):
        tiles[OWN, 4 + k : 5 + k, :] = nbr_ref[k, 0, 0].astype(F32)

    for layer, (b_ref, r_ref, m_ref) in enumerate(((b1_ref, r1_ref, m1_ref), (b2_ref, r2_ref, m2_ref))):
        basis = b_ref[...].astype(F32)
        win[layer] = padded_t(basis)[0:RHID, 0:16].astype(BF16)
        winp[layer] = jnp.concatenate([basis, jnp.zeros_like(basis)], axis=0).astype(BF16)
        for l in range(3):
            block = r_ref[:, l * CHAN : (l + 1) * CHAN].astype(F32)
            wout[layer, l * CHAN : (l + 1) * CHAN, :] = padded_t(block)[:, 0:RHID].astype(BF16)
            block = m_ref[l * CHAN : (l + 1) * CHAN, :].astype(F32)
            mix[layer, :, l * CHAN : (l + 1) * CHAN] = block.T.astype(BF16)
    cut[...] = cu_ref[...].astype(F32).T.astype(BF16)
    emb = jnp.concatenate([emb_ref[...], jnp.zeros((3, CHAN), F32)], axis=0)
    emb_hi = emb.astype(BF16).astype(F32)
    both = jnp.concatenate([emb_hi, emb - emb_hi], axis=0)
    embt[...] = padded_t(both)[:, 0:16].astype(BF16)
    for layer, ro_ref in enumerate((ro1_ref, ro2_ref)):
        rocol[layer] = jnp.broadcast_to(ro_ref[...].reshape(1, CHAN), (LANES, CHAN)).T

    tpos[...] = jnp.zeros_like(tpos)
    tnb[...] = jnp.zeros_like(tnb)

    pl.semaphore_wait(barrier, len(DIRS))
    copies = []
    for n, (f, dy, dz) in enumerate(DIRS):
        copy = pltpu.make_async_remote_copy(
            src_ref=tiles.at[OWN],
            dst_ref=tiles.at[cell_number(f, -dy, -dz)],
            send_sem=send_a.at[n],
            recv_sem=recv_a.at[n],
            device_id=device(f, dy, dz),
            device_id_type=MESH,
        )
        copy.start()
        copies.append(copy)
    sigma_f = sigma.astype(F32)
    row8 = lax.broadcasted_iota(jnp.int32, (8, LANES), 0)
    row16 = lax.broadcasted_iota(jnp.int32, (16, LANES), 0)
    rowf = lax.broadcasted_iota(jnp.int32, (LANES, LANES), 0).astype(F32)
    spec16 = jnp.where(row16 < 8, row16, row16 - 8).astype(F32)
    basis_centre = row8.astype(F32) * (1.0 / 7.0)

    def tables(first, last, pairs):
        @pl.loop(first, last)
        def _(c):
            top = tiles[c, 0:8, :]
            high = top.astype(BF16).astype(F32)
            low = pltpu.roll(top - high, 4, 0)
            pg[pl.ds(pl.multiple_of(c * 8, 8), 8), 0:LANES] = jnp.where(row8 < 4, high, low)
            entries = tiles[c, 4:16, :]
            codes = jnp.floor((entries + 0.5) * (1.0 / LANES))
            start = pl.multiple_of(c * 24, 8)
            prt[pl.ds(start, 24), :] = jnp.concatenate([codes, entries - LANES * codes], axis=0)

        low, high = pairs
        tpos[low * 8 : high * 8, :] = pg[low * 8 : high * 8, 0:LANES].astype(BF16)
        tnb[low * 24 : high * 24, :] = prt[low * 24 : high * 24, :].astype(BF16)

    for j in range(BLOCKS):
        rows = con_ref[j]
        own_slot = jnp.where(sigma_f > 0, rows[0:1], rows[1:2])
        oh[j, :, PAIRS:] = (rowf == own_slot).astype(BF16)
        ident = jnp.where(own_slot < 0, -1.0, rows[2:3] * LANES + own_slot)
        column[j] = jnp.broadcast_to(ident, (LANES, LANES)).T

    def centres(j):
        rows = con_ref[j]
        cell = jnp.broadcast_to(rows[2:3], (8, LANES))
        hot = oh[j, :, PAIRS:]
        pg[:, 0:LANES] = dot(tpos[...], hot)
        prt[0 : CELLS * 24 + 24, :] = dot(tnb[...], hot)
        acc = [jnp.zeros((8, LANES), F32) for _ in range(4)]
        for c in range(CELLS):
            here = cell == float(c)
            acc[0] = jnp.where(here, pg[c * 8 : c * 8 + 8, 0:LANES], acc[0])
            for part in range(3):
                rows_at = c * 24 + part * 8
                acc[1 + part] = jnp.where(here, prt[rows_at : rows_at + 8, :], acc[1 + part])
        both = jnp.concatenate(acc[1:], axis=0)
        cpos[j] = acc[0] + pltpu.roll(acc[0], 4, 0)
        code[j] = both[0:12]
        slot[j] = both[12:24]

    def geometry(j):
        rows = con_ref[j]
        codes, slots = code[j], slot[j]
        nine = jnp.floor((codes + 0.5) * (1.0 / 9.0))
        three = jnp.floor((codes + 0.5) * (1.0 / 3.0))
        step_x = nine - 1.0
        step_y = three - 3.0 * nine - 1.0
        step_z = codes - 3.0 * three - 1.0
        target = rows[2:3] + 9.0 * sigma_f * step_x + 3.0 * step_y + step_z
        tcell[j, 0:12] = target
        tcell[j, 12:13] = rows[2:3]
        for k in range(NEIGH):
            oh[j, :, k * LANES : (k + 1) * LANES] = (rowf == slots[k : k + 1]).astype(BF16)
        for h in range(PAIRS // 256):
            lanes = slice(h * 256, (h + 1) * 256)
            pg[:, lanes] = dot(tpos[...], oh[j, :, lanes])
        for k in range(NEIGH):
            lanes = slice(k * LANES, (k + 1) * LANES)
            here = jnp.broadcast_to(target[k : k + 1], (8, LANES))
            acc = jnp.zeros((8, LANES), F32)
            for c in range(CELLS):
                acc = jnp.where(here == float(c), pg[c * 8 : c * 8 + 8, lanes], acc)
            gs[k * 8 : (k + 1) * 8, :] = acc + pltpu.roll(acc, 4, 0)
        centre = cpos[j]
        x = (gs[pl.ds(0, 12, stride=8), :] + 10.0 * step_x - centre[0:1]) / 5.0
        y = (gs[pl.ds(1, 12, stride=8), :] + 10.0 * step_y - centre[1:2]) / 5.0
        z = (gs[pl.ds(2, 12, stride=8), :] + 10.0 * step_z - centre[2:3]) / 5.0
        species = gs[pl.ds(3, 12, stride=8), :]
        s = x * x + y * y + z * z
        inside = jnp.maximum(1.0 - s, 0.0)
        alive = inside * (species > -0.5).astype(F32)
        env = inside * alive
        geo[j, 0] = x
        geo[j, 1] = y
        geo[j, 2] = z
        geo[j, 3] = env
        geo[j, 4] = alive
        harm = [
            env,
            env * (ROOT3 * x),
            env * (ROOT3 * y),
            env * (ROOT3 * z),
            env * (ROOT15 * x * y),
            env * (ROOT15 * y * z),
            env * (0.5 * ROOT5 * (3.0 * z * z - s)),
            env * (ROOT15 * x * z),
            env * (0.5 * ROOT15 * (x * x - y * y)),
        ]
        for k in range(NEIGH):
            lanes = slice(k * LANES, (k + 1) * LANES)
            for m in range(9):
                yb[j, k, m] = jnp.broadcast_to(harm[m][k : k + 1], (8, LANES))
            t = (jnp.broadcast_to(s[k : k + 1], (8, LANES)) - basis_centre) * 7.0
            e = jnp.exp(-(t * t))
            rb[j, :, lanes] = jnp.concatenate([e, e], axis=0).astype(BF16)
            rbd[j, :, lanes] = e * (-14.0 * t)
            spoh[j, :, lanes] = (spec16 == species[k : k + 1]).astype(BF16)

    def radial(layer, j, at):
        for h in range(PAIRS // 256):
            lanes = slice(h * 256, (h + 1) * 256)
            pre = dot(win[layer], rb[j, :, lanes])
            sig = sigmoid(pre)
            hid = pre * sig
            ds[at, :, lanes] = sig + hid * (1.0 - sig)
            out = dot(wout[layer], hid.astype(BF16))
            g[at, 2 * h] = out[:, 0:LANES]
            g[at, 2 * h + 1] = out[:, LANES:]

    def gather_sum(j, at, second):
        @pl.loop(0, CHAN // 16)
        def _(ct):
            starts = [pl.multiple_of(ct * 16 + 8 * n, 8) for n in range(2)]
            acc = [[None] * 9 for _ in range(2)]
            for k in range(NEIGH):
                harm = [yb[j, k, m] for m in range(9)]
                for n in range(2):
                    f = feat[at, k, pl.ds(starts[n], 8), :]
                    for l, (low, high) in enumerate(DEGREES):
                        here = pl.ds(pl.multiple_of(l * CHAN + starts[n], 8), 8)
                        value = g[at, k, here, :] * f
                        if not second:
                            g[at, k, here, :] = value
                        for m in range(low, high):
                            term = value * harm[m]
                            acc[n][m] = term if k == 0 else acc[n][m] + term
            for n in range(2):
                sums = [a * SCALE for a in acc[n]]
                for m in range(9):
                    a_s[at, m, pl.ds(starts[n], 8), :] = sums[m]
                one = sums[1] * sums[1] + sums[2] * sums[2] + sums[3] * sums[3]
                two = sums[4] * sums[4] + sums[5] * sums[5] + sums[6] * sums[6]
                two = two + sums[7] * sums[7] + sums[8] * sums[8]
                for l, value in enumerate((sums[0], one, two)):
                    inv[pl.ds(pl.multiple_of(l * CHAN + starts[n], 8), 8), :] = value

    def sums_back(layer, at, dpre):
        dinv = dot(mix_refs[layer][...], dpre.astype(BF16))
        da[0] = SCALE * dinv[0:CHAN]
        for l, (low, high) in enumerate(DEGREES[1:], 1):
            part = (2.0 * SCALE) * dinv[l * CHAN : (l + 1) * CHAN]
            for m in range(low, high):
                da[m] = a_s[at, m] * part

    def pair_back(layer, j, at, second):
        for h in range(NEIGH // 2):
            for half in range(2):
                k = 2 * h + half
                lanes = slice(half * LANES, (half + 1) * LANES)
                harm = [yb[j, k, m] for m in range(9)]
                sums = [None] * 9
                for ct in range(0, CHAN // 8, 2):
                    df, dvals = [], [[], [], []]
                    for n in range(2):
                        chans = slice((ct + n) * 8, (ct + n + 1) * 8)
                        f = feat[at, k, chans, :]
                        cots = [da[m, chans, :] for m in range(9)]
                        for l, (low, high) in enumerate(DEGREES):
                            r = g[at, k, l * CHAN + (ct + n) * 8 : l * CHAN + (ct + n + 1) * 8, :]
                            value = r * f if second else r
                            dval = None
                            for m in range(low, high):
                                part = cots[m] * value
                                sums[m] = part if sums[m] is None else sums[m] + part
                                part = cots[m] * harm[m]
                                dval = part if dval is None else dval + part
                            dvals[l].append(dval * f)
                            if second:
                                df_l = dval * r
                                if l == 0:
                                    df.append(df_l)
                                else:
                                    df[n] = df[n] + df_l
                    for l in range(3):
                        rows = slice(l * CHAN + ct * 8, l * CHAN + ct * 8 + 16)
                        dr[h % 2, rows, lanes] = jnp.concatenate(dvals[l], axis=0).astype(BF16)
                    if second:
                        chans = slice(ct * 8, ct * 8 + 16)
                        dfe[chans, k * LANES : (k + 1) * LANES] = jnp.concatenate(df, axis=0).astype(BF16)
                for m in range(9):
                    prt[m * 96 + k * 8 : m * 96 + k * 8 + 8, :] = sums[m]
            lanes = slice(h * 256, (h + 1) * 256)
            dhid = dot(radial_refs[layer][...], dr[h % 2])
            dpr[:, lanes] = (dhid * ds[at, :, lanes]).astype(BF16)
        for h in range(NEIGH // 2):
            lanes = slice(h * 256, (h + 1) * 256)
            drb = dot(winp[layer], dpr[:, lanes])[0:8] * rbd[j, :, lanes]
            q[h * 16 : h * 16 + 8, :] = drb[:, 0:LANES]
            q[h * 16 + 8 : h * 16 + 16, :] = drb[:, LANES:]

    def eight(ref, base):
        total = ref[pl.ds(base, 12, stride=8), :]
        for r in range(1, 8):
            total = total + ref[pl.ds(base + r, 12, stride=8), :]
        return total

    def geometry_back(j):
        x, y, z, env, alive = (geo[j, n] for n in range(5))
        s = x * x + y * y + z * z
        d = [eight(prt, m * 96) for m in range(9)]
        harm = [
            None,
            ROOT3 * x,
            ROOT3 * y,
            ROOT3 * z,
            ROOT15 * x * y,
            ROOT15 * y * z,
            0.5 * ROOT5 * (3.0 * z * z - s),
            ROOT15 * x * z,
            0.5 * ROOT15 * (x * x - y * y),
        ]
        denv = d[0]
        for m in range(1, 9):
            denv = denv + d[m] * harm[m]
        dsq = eight(q, 0) - 2.0 * denv * alive
        d = [None] + [env * value for value in d[1:]]
        d6 = ROOT5 * d[6]
        dx = 2.0 * x * dsq + ROOT3 * d[1] + ROOT15 * (y * d[4] + z * d[7] + x * d[8]) - x * d6
        dy = 2.0 * y * dsq + ROOT3 * d[2] + ROOT15 * (x * d[4] + z * d[5] - y * d[8]) - y * d6
        dz = 2.0 * z * dsq + ROOT3 * d[3] + ROOT15 * (y * d[5] + x * d[7]) + 2.0 * z * d6
        return dx, dy, dz

    radial_refs = (r1_ref, r2_ref)
    mix_refs = (m1_ref, m2_ref)

    def arrive(far):
        for n, d in enumerate(DIRS):
            if (d[0] == 0) == far:
                copy = copies[n]
                copy.wait_recv()

    arrive(False)
    for c in (8, CELLS):
        pg[c * 8 : c * 8 + 8, 0:LANES] = jnp.zeros((8, LANES), F32)
        prt[c * 24 : c * 24 + 24, :] = jnp.zeros((24, LANES), F32)
    tables(9, CELLS, (8, CELLS + 1))

    @pl.loop(0, BLOCKS)
    def _(i):
        j = lax.rem(i + FAR_BLOCKS, BLOCKS)

        @pl.when(i == BLOCKS - FAR_BLOCKS)
        def _():
            arrive(True)
            tables(0, 10, (0, 10))

        centres(j)

        @pl.when(j == 0)
        def _():
            cpos[0] = tiles[OWN, 0:8, :]

        geometry(j)
        for h in range(PAIRS // 256):
            out = dot(embt[...], spoh[j, :, h * 256 : (h + 1) * 256])
            feat[j, 2 * h] = out[:, 0:LANES]
            feat[j, 2 * h + 1] = out[:, LANES:]
        radial(0, j, j)
        gather_sum(j, j, False)
        pre = dot(mix[0], inv[...].astype(BF16))
        sig = sigmoid(pre)
        value = pre * sig
        dnode[j] = sig + value * (1.0 - sig)
        hot = (spec16 == cpos[j, 3:4, :]).astype(BF16)
        state = value + dot(embt[...], hot)
        node[j] = state
        upd[:, pl.ds(pl.multiple_of(j * LANES, LANES), LANES)] = dot(cut[...], state.astype(BF16)).astype(BF16)

    for k in range(NEIGH):
        lanes = slice(k * LANES, (k + 1) * LANES)
        ident = tcell[0, k : k + 1, :] * LANES + slot[0, k : k + 1, :]
        for j in range(BLOCKS):
            oh_site[j * LANES : (j + 1) * LANES, lanes] = (column[j] == ident).astype(BF16)

    radial(1, 0, BLOCKS)
    for h in range(PAIRS // 256):
        out = dot(upd[...], oh_site[:, h * 256 : (h + 1) * 256])
        feat[BLOCKS, 2 * h] = out[:, 0:LANES]
        feat[BLOCKS, 2 * h + 1] = out[:, LANES:]
    gather_sum(0, BLOCKS, True)
    live = (cpos[0, 3:4, :] > -0.5).astype(F32)
    pre = dot(mix[1], inv[...].astype(BF16))
    sig = sigmoid(pre)
    value = pre * sig
    energy = jnp.sum(rocol[0] * node[0] + rocol[1] * value, axis=0, keepdims=True)
    en_ref[0, 0] = live * energy

    sums_back(1, BLOCKS, rocol[1] * live * (sig + value * (1.0 - sig)))
    pair_back(1, 0, BLOCKS, True)
    for m, value in enumerate(geometry_back(0)):
        gacc[0, m] = value
    gacc[1:] = jnp.zeros((BLOCKS - 1, 3, NEIGH, LANES), F32)
    for h in range(BLOCKS // 2):
        rows = slice(h * 256, (h + 1) * 256)
        dupd[:, rows] = dot_nt(dfe[...], oh_site[rows, :]).astype(BF16)
    for j in range(BLOCKS):
        back = dot(cu_ref[...], dupd[:, j * LANES : (j + 1) * LANES])
        if j == 0:
            back = back + rocol[0] * live
        node[j] = back

    returns = []
    for n, (f, dy, dz) in enumerate(DIRS):
        returns.append(
            pltpu.make_async_remote_copy(
                src_ref=gsend.at[cell_number(f, dy, dz)],
                dst_ref=grecv.at[cell_number(f, -dy, -dz)],
                send_sem=send_d.at[n],
                recv_sem=recv_d.at[n],
                device_id=device(f, dy, dz),
                device_id_type=MESH,
            )
        )

    def depart(far):
        @pl.loop(0 if far else 9, 9 if far else CELLS)
        def _(c):
            rows = sc[pl.ds(pl.multiple_of(c * 8, 8), 8), :]
            gsend[c] = rows + pltpu.roll(rows, 4, 0)

        for n, d in enumerate(DIRS):
            if (d[0] == 0) == far:
                copy = returns[n]
                copy.start()

    sc[...] = jnp.zeros_like(sc)

    @pl.loop(0, BLOCKS)
    def _(j):
        sums_back(0, j, node[j] * dnode[j])
        pair_back(0, j, j, False)
        parts = []
        for m, value in enumerate(geometry_back(j)):
            value = (value + gacc[j, m]) * 0.2
            whole = jnp.concatenate([value, -jnp.sum(value, axis=0, keepdims=True)], axis=0)
            high = whole.astype(BF16).astype(F32)
            parts.append((high, whole - high))
        for k in range(NEIGH + 1):
            tile = jnp.zeros((8, LANES), F32)
            for m in range(3):
                for n in range(2):
                    tile = jnp.where(row8 == m + 4 * n, parts[m][n][k : k + 1], tile)
            where = jnp.broadcast_to(tcell[j, k : k + 1, :], (8, LANES))
            lanes = slice(k * LANES, (k + 1) * LANES)
            for c in range(0, CELLS + 1, 2):
                pair = [jnp.where(where == float(c + n), tile, 0.0) for n in range(2)]
                ml[c * 8 : c * 8 + 16, lanes] = jnp.concatenate(pair, axis=0).astype(BF16)
        sc[...] += dot_nt(ml[...], oh[j])

        @pl.when(j == FAR_BLOCKS - 1)
        def _():
            depart(True)

    depart(False)
    for copy in copies:
        copy.wait_send()
    for copy in returns:
        copy.wait_recv()
    total = gsend[OWN]
    for d in DIRS:
        total = total + grecv[cell_number(*d)]
    for m in range(3):
        fo_ref[m, 0, 0] = -total[m : m + 1]
    for copy in returns:
        copy.wait_send()


def body(sizes, positions, species, neighbours, *weights):
    table = jnp.asarray(site_table())
    vmem = pl.BlockSpec(memory_space=pltpu.VMEM)
    n = len(DIRS)
    scratch = [
        pltpu.VMEM((CELLS, 16, LANES), F32),
        pltpu.VMEM((CELLS * 8 + 8, LANES), BF16),
        pltpu.VMEM((CELLS * 24 + 24, LANES), BF16),
        pltpu.VMEM((CELLS, 8, LANES), F32),
        pltpu.VMEM((CELLS, 8, LANES), F32),
        pltpu.VMEM((BLOCKS, 8, LANES), F32),
        pltpu.VMEM((BLOCKS, NEIGH, LANES), F32),
        pltpu.VMEM((BLOCKS, NEIGH, LANES), F32),
        pltpu.VMEM((BLOCKS, 16, LANES), F32),
        pltpu.VMEM((BLOCKS, LANES, PAIRS + LANES), BF16),
        pltpu.VMEM((BLOCKS * LANES, PAIRS), BF16),
        pltpu.VMEM((CELLS * 8 + 8, PAIRS), F32),
        pltpu.VMEM((96, LANES), F32),
        pltpu.VMEM((BLOCKS, LANES, LANES), F32),
        pltpu.VMEM((BLOCKS, 5, NEIGH, LANES), F32),
        pltpu.VMEM((BLOCKS, NEIGH, 9, 8, LANES), F32),
        pltpu.VMEM((BLOCKS, 16, PAIRS), BF16),
        pltpu.VMEM((BLOCKS, 8, PAIRS), F32),
        pltpu.VMEM((BLOCKS, 16, PAIRS), BF16),
        pltpu.VMEM((BLOCKS + 1, NEIGH, 3 * CHAN, LANES), F32),
        pltpu.VMEM((BLOCKS + 1, NEIGH, CHAN, LANES), F32),
        pltpu.VMEM((BLOCKS + 1, RHID, PAIRS), F32),
        pltpu.VMEM((BLOCKS + 1, 9, CHAN, LANES), F32),
        pltpu.VMEM((3 * CHAN, LANES), F32),
        pltpu.VMEM((BLOCKS, CHAN, LANES), F32),
        pltpu.VMEM((BLOCKS, CHAN, LANES), F32),
        pltpu.VMEM((CHAN, BLOCKS * LANES), BF16),
        pltpu.VMEM((CHAN, BLOCKS * LANES), BF16),
        pltpu.VMEM((9, CHAN, LANES), F32),
        pltpu.VMEM((2, 3 * CHAN, 2 * LANES), BF16),
        pltpu.VMEM((CHAN, PAIRS), BF16),
        pltpu.VMEM((BLOCKS, 3, NEIGH, LANES), F32),
        pltpu.VMEM((9 * 96, LANES), F32),
        pltpu.VMEM((96, LANES), F32),
        pltpu.VMEM((CELLS * 8 + 8, PAIRS + LANES), BF16),
        pltpu.VMEM((CELLS * 8 + 8, LANES), F32),
        pltpu.VMEM((RHID, PAIRS), BF16),
        pltpu.VMEM((2, RHID, 16), BF16),
        pltpu.VMEM((2, 3 * CHAN, RHID), BF16),
        pltpu.VMEM((2, CHAN, 3 * CHAN), BF16),
        pltpu.VMEM((CHAN, CHAN), BF16),
        pltpu.VMEM((CHAN, 16), BF16),
        pltpu.VMEM((2, 16, RHID), BF16),
        pltpu.VMEM((2, CHAN, LANES), F32),
    ] + [pltpu.SemaphoreType.DMA((n,))] * 4
    return pl.pallas_call(
        functools.partial(kernel, sizes),
        out_shape=(
            jax.ShapeDtypeStruct(species.shape, F32),
            jax.ShapeDtypeStruct(positions.shape, F32),
        ),
        in_specs=[vmem] * 14,
        out_specs=(vmem, vmem),
        scratch_shapes=scratch,
        compiler_params=pltpu.CompilerParams(
            collective_id=0, has_side_effects=True, vmem_limit_bytes=56 << 20
        ),
    )(positions, species, neighbours, *weights, table)


def solution(mesh):
    sizes = tuple(mesh.shape[axis] for axis in ("gx", "gy", "gz"))
    grid = ("gx", "gy", "gz", None)
    return jax.shard_map(
        functools.partial(body, sizes),
        mesh=mesh,
        in_specs=(P(None, *grid), P(*grid), P(None, *grid)) + (P(),) * 10,
        out_specs=(P(*grid), P(None, *grid)),
        check_vma=False,
    )
```

```python
import functools
import itertools
import math

import jax
import jax.numpy as jnp
import numpy as np
from jax import lax
from jax.experimental import pallas as pl
from jax.experimental.pallas import tpu as pltpu
from jax.sharding import PartitionSpec as P

MESH = pl.DeviceIdType.MESH
F32 = jnp.float32
BF16 = jnp.bfloat16
LANES = 128
CHAN = 128
RHID = 64
NEIGH = 12
CELLS = 27
N_INPUTS = 14
OWN = 13
BLOCKS = 6
FAR_BLOCKS = 4
PAIRS = NEIGH * LANES
ROOT3 = math.sqrt(3.0)
ROOT5 = math.sqrt(5.0)
ROOT15 = math.sqrt(15.0)
SCALE = 1.0 / math.sqrt(NEIGH)
DEGREES = ((0, 1), (1, 4), (4, 9))
DIRS = [d for d in itertools.product(range(3), (-1, 0, 1), (-1, 0, 1)) if d != (1, 0, 0)]
DIRS.sort(key=lambda d: (d[0], -abs(d[1]) - abs(d[2])))


def cell_number(f, dy, dz):
    return f * 9 + (dy + 1) * 3 + dz + 1


def site_table():
    sites = []
    depth = {-1: (3, 4), 0: range(5), 1: (0, 1)}
    for f, dy, dz in itertools.product(range(3), (-1, 0, 1), (-1, 0, 1)):
        if (f, dy, dz) == (1, 0, 0):
            continue
        for tx, ty, tz in itertools.product(depth[f - 1], depth[dy], depth[dz]):
            rest = ty * 5 + tz
            sites.append(((f - 1) * 5 + tx, tx * 25 + rest, (4 - tx) * 25 + rest, cell_number(f, dy, dz)))
    sites.sort(key=lambda s: -s[0])
    near = (BLOCKS - FAR_BLOCKS) * LANES
    sites = sites[near:][::-1] + [None] * (BLOCKS * LANES - LANES - len(sites)) + sites[:near]
    table = np.zeros((BLOCKS, 8, LANES), np.float32)
    table[:, 0:2] = -1.0
    table[:, 2] = OWN
    table[0, 0:2] = np.arange(LANES)
    for n, site in enumerate(sites):
        if site is not None:
            table[1 + n // LANES, 0:3, n % LANES] = site[1:]
    return table


def dot(a, b):
    return jnp.dot(a, b, preferred_element_type=F32)


def dot_nt(a, b):
    return lax.dot_general(a, b, (((1,), (1,)), ((), ())), preferred_element_type=F32)


def sigmoid(v):
    return 0.5 * jnp.tanh(0.5 * v) + 0.5


def padded_t(value):
    rows, columns = value.shape
    if rows < LANES:
        value = jnp.concatenate([value, jnp.zeros((LANES - rows, columns), F32)], axis=0)
    if columns < LANES:
        value = jnp.concatenate([value, jnp.zeros((LANES, LANES - columns), F32)], axis=1)
    return value.T


def kernel(
    sizes,
    *refs,
):
    n = N_INPUTS
    work(sizes, refs[:n], refs[n], refs[n + 1 : 2 * n + 1], refs[2 * n + 1], *refs[2 * n + 2 :])


def work(
    sizes, sources, out_ref, inputs, input_sem,
    tiles, tpos, tnb, gsend, grecv,
    cpos, code, slot, tcell, oh, oh_site, pg, gs, column, geo, yb, rb, rbd, spoh,
    g, feat, ds, a_s, inv, node, dnode, upd, dupd, da, dr, dfe, gacc, prt, q, ml, sc, dpr,
    win, wout, mix, cut, embt, winp, rocol,
    send_a, recv_a, send_d, recv_d,
):
    (pos_ref, spc_ref, nbr_ref, emb_ref, b1_ref, r1_ref, m1_ref, ro1_ref,
     b2_ref, r2_ref, m2_ref, ro2_ref, cu_ref, con_ref) = inputs
    nx, ny, nz = sizes
    gx, gy, gz = lax.axis_index("gx"), lax.axis_index("gy"), lax.axis_index("gz")
    sigma = 1 - 2 * lax.rem(gx, 2)

    def device(f, dy, dz):
        return (
            lax.rem(gx + (f - 1) * sigma + nx, nx),
            lax.rem(gy + dy + ny, ny),
            lax.rem(gz + dz + nz, nz),
        )

    barrier = pltpu.get_barrier_semaphore()
    for d in DIRS:
        pl.semaphore_signal(barrier, inc=1, device_id=device(*d), device_id_type=MESH)

    fetches = []
    for n in range(N_INPUTS):
        fetch = pltpu.make_async_copy(sources[n], inputs[n], input_sem.at[n])
        fetch.start()
        fetches.append(fetch)
    for fetch in fetches:
        fetch.wait()

    for m in range(3):
        tiles[OWN, m : m + 1, :] = pos_ref[m, 0, 0]
    tiles[OWN, 3:4, :] = spc_ref[0, 0].astype(F32)
    for k in range(NEIGH):
        tiles[OWN, 4 + k : 5 + k, :] = nbr_ref[k, 0, 0].astype(F32)

    for layer, (b_ref, r_ref, m_ref) in enumerate(((b1_ref, r1_ref, m1_ref), (b2_ref, r2_ref, m2_ref))):
        basis = b_ref[...].astype(F32)
        win[layer] = padded_t(basis)[0:RHID, 0:16].astype(BF16)
        winp[layer] = jnp.concatenate([basis, jnp.zeros_like(basis)], axis=0).astype(BF16)
        for l in range(3):
            block = r_ref[:, l * CHAN : (l + 1) * CHAN].astype(F32)
            wout[layer, l * CHAN : (l + 1) * CHAN, :] = padded_t(block)[:, 0:RHID].astype(BF16)
            block = m_ref[l * CHAN : (l + 1) * CHAN, :].astype(F32)
            mix[layer, :, l * CHAN : (l + 1) * CHAN] = block.T.astype(BF16)
    cut[...] = cu_ref[...].astype(F32).T.astype(BF16)
    emb = jnp.concatenate([emb_ref[...], jnp.zeros((3, CHAN), F32)], axis=0)
    emb_hi = emb.astype(BF16).astype(F32)
    both = jnp.concatenate([emb_hi, emb - emb_hi], axis=0)
    embt[...] = padded_t(both)[:, 0:16].astype(BF16)
    for layer, ro_ref in enumerate((ro1_ref, ro2_ref)):
        rocol[layer] = jnp.broadcast_to(ro_ref[...].reshape(1, CHAN), (LANES, CHAN)).T

    tpos[...] = jnp.zeros_like(tpos)
    tnb[...] = jnp.zeros_like(tnb)

    pl.semaphore_wait(barrier, len(DIRS))
    copies = []
    for n, (f, dy, dz) in enumerate(DIRS):
        copy = pltpu.make_async_remote_copy(
            src_ref=tiles.at[OWN],
            dst_ref=tiles.at[cell_number(f, -dy, -dz)],
            send_sem=send_a.at[n],
            recv_sem=recv_a.at[n],
            device_id=device(f, dy, dz),
            device_id_type=MESH,
        )
        copy.start()
        copies.append(copy)
    sigma_f = sigma.astype(F32)
    row8 = lax.broadcasted_iota(jnp.int32, (8, LANES), 0)
    row16 = lax.broadcasted_iota(jnp.int32, (16, LANES), 0)
    rowf = lax.broadcasted_iota(jnp.int32, (LANES, LANES), 0).astype(F32)
    spec16 = jnp.where(row16 < 8, row16, row16 - 8).astype(F32)
    basis_centre = row8.astype(F32) * (1.0 / 7.0)

    def tables(first, last, pairs):
        @pl.loop(first, last)
        def _(c):
            top = tiles[c, 0:8, :]
            high = top.astype(BF16).astype(F32)
            low = pltpu.roll(top - high, 4, 0)
            pg[pl.ds(pl.multiple_of(c * 8, 8), 8), 0:LANES] = jnp.where(row8 < 4, high, low)
            entries = tiles[c, 4:16, :]
            codes = jnp.floor((entries + 0.5) * (1.0 / LANES))
            start = pl.multiple_of(c * 24, 8)
            prt[pl.ds(start, 24), :] = jnp.concatenate([codes, entries - LANES * codes], axis=0)

        low, high = pairs
        tpos[low * 8 : high * 8, :] = pg[low * 8 : high * 8, 0:LANES].astype(BF16)
        tnb[low * 24 : high * 24, :] = prt[low * 24 : high * 24, :].astype(BF16)

    for j in range(BLOCKS):
        rows = con_ref[j]
        own_slot = jnp.where(sigma_f > 0, rows[0:1], rows[1:2])
        oh[j, :, PAIRS:] = (rowf == own_slot).astype(BF16)
        ident = jnp.where(own_slot < 0, -1.0, rows[2:3] * LANES + own_slot)
        column[j] = jnp.broadcast_to(ident, (LANES, LANES)).T

    def centres(j):
        rows = con_ref[j]
        cell = jnp.broadcast_to(rows[2:3], (8, LANES))
        hot = oh[j, :, PAIRS:]
        pg[:, 0:LANES] = dot(tpos[...], hot)
        prt[0 : CELLS * 24 + 24, :] = dot(tnb[...], hot)
        acc = [jnp.zeros((8, LANES), F32) for _ in range(4)]
        for c in range(CELLS):
            here = cell == float(c)
            acc[0] = jnp.where(here, pg[c * 8 : c * 8 + 8, 0:LANES], acc[0])
            for part in range(3):
                rows_at = c * 24 + part * 8
                acc[1 + part] = jnp.where(here, prt[rows_at : rows_at + 8, :], acc[1 + part])
        both = jnp.concatenate(acc[1:], axis=0)
        cpos[j] = acc[0] + pltpu.roll(acc[0], 4, 0)
        code[j] = both[0:12]
        slot[j] = both[12:24]

    def geometry(j):
        rows = con_ref[j]
        codes, slots = code[j], slot[j]
        nine = jnp.floor((codes + 0.5) * (1.0 / 9.0))
        three = jnp.floor((codes + 0.5) * (1.0 / 3.0))
        step_x = nine - 1.0
        step_y = three - 3.0 * nine - 1.0
        step_z = codes - 3.0 * three - 1.0
        target = rows[2:3] + 9.0 * sigma_f * step_x + 3.0 * step_y + step_z
        tcell[j, 0:12] = target
        tcell[j, 12:13] = rows[2:3]
        for k in range(NEIGH):
            oh[j, :, k * LANES : (k + 1) * LANES] = (rowf == slots[k : k + 1]).astype(BF16)
        for h in range(PAIRS // 256):
            lanes = slice(h * 256, (h + 1) * 256)
            pg[:, lanes] = dot(tpos[...], oh[j, :, lanes])
        for k in range(NEIGH):
            lanes = slice(k * LANES, (k + 1) * LANES)
            here = jnp.broadcast_to(target[k : k + 1], (8, LANES))
            acc = jnp.zeros((8, LANES), F32)
            for c in range(CELLS):
                acc = jnp.where(here == float(c), pg[c * 8 : c * 8 + 8, lanes], acc)
            gs[k * 8 : (k + 1) * 8, :] = acc + pltpu.roll(acc, 4, 0)
        centre = cpos[j]
        x = (gs[pl.ds(0, 12, stride=8), :] + 10.0 * step_x - centre[0:1]) / 5.0
        y = (gs[pl.ds(1, 12, stride=8), :] + 10.0 * step_y - centre[1:2]) / 5.0
        z = (gs[pl.ds(2, 12, stride=8), :] + 10.0 * step_z - centre[2:3]) / 5.0
        species = gs[pl.ds(3, 12, stride=8), :]
        s = x * x + y * y + z * z
        inside = jnp.maximum(1.0 - s, 0.0)
        alive = inside * (species > -0.5).astype(F32)
        env = inside * alive
        geo[j, 0] = x
        geo[j, 1] = y
        geo[j, 2] = z
        geo[j, 3] = env
        geo[j, 4] = alive
        harm = [
            env,
            env * (ROOT3 * x),
            env * (ROOT3 * y),
            env * (ROOT3 * z),
            env * (ROOT15 * x * y),
            env * (ROOT15 * y * z),
            env * (0.5 * ROOT5 * (3.0 * z * z - s)),
            env * (ROOT15 * x * z),
            env * (0.5 * ROOT15 * (x * x - y * y)),
        ]
        for k in range(NEIGH):
            lanes = slice(k * LANES, (k + 1) * LANES)
            for m in range(9):
                yb[j, k, m] = jnp.broadcast_to(harm[m][k : k + 1], (8, LANES))
            t = (jnp.broadcast_to(s[k : k + 1], (8, LANES)) - basis_centre) * 7.0
            e = jnp.exp(-(t * t))
            rb[j, :, lanes] = jnp.concatenate([e, e], axis=0).astype(BF16)
            rbd[j, :, lanes] = e * (-14.0 * t)
            spoh[j, :, lanes] = (spec16 == species[k : k + 1]).astype(BF16)

    def radial(layer, j, at):
        for h in range(PAIRS // 256):
            lanes = slice(h * 256, (h + 1) * 256)
            pre = dot(win[layer], rb[j, :, lanes])
            sig = sigmoid(pre)
            hid = pre * sig
            ds[at, :, lanes] = sig + hid * (1.0 - sig)
            out = dot(wout[layer], hid.astype(BF16))
            g[at, 2 * h] = out[:, 0:LANES]
            g[at, 2 * h + 1] = out[:, LANES:]

    def gather_sum(j, at, second):
        for ct in range(CHAN // 16):
            starts = [ct * 16 + 8 * n for n in range(2)]
            acc = [[None] * 9 for _ in range(2)]
            for k in range(NEIGH):
                harm = [yb[j, k, m] for m in range(9)]
                for n in range(2):
                    f = feat[at, k, pl.ds(starts[n], 8), :]
                    for l, (low, high) in enumerate(DEGREES):
                        here = pl.ds(l * CHAN + starts[n], 8)
                        value = g[at, k, here, :] * f
                        if not second:
                            g[at, k, here, :] = value
                        for m in range(low, high):
                            term = value * harm[m]
                            acc[n][m] = term if k == 0 else acc[n][m] + term
            for n in range(2):
                sums = [a * SCALE for a in acc[n]]
                for m in range(9):
                    a_s[at, m, pl.ds(starts[n], 8), :] = sums[m]
                one = sums[1] * sums[1] + sums[2] * sums[2] + sums[3] * sums[3]
                two = sums[4] * sums[4] + sums[5] * sums[5] + sums[6] * sums[6]
                two = two + sums[7] * sums[7] + sums[8] * sums[8]
                for l, value in enumerate((sums[0], one, two)):
                    inv[pl.ds(l * CHAN + starts[n], 8), :] = value

    def sums_back(layer, at, dpre):
        dinv = dot(mix_refs[layer][...], dpre.astype(BF16))
        da[0] = SCALE * dinv[0:CHAN]
        for l, (low, high) in enumerate(DEGREES[1:], 1):
            part = (2.0 * SCALE) * dinv[l * CHAN : (l + 1) * CHAN]
            for m in range(low, high):
                da[m] = a_s[at, m] * part

    def pair_back(layer, j, at, second):
        for h in range(NEIGH // 2):
            for half in range(2):
                k = 2 * h + half
                lanes = slice(half * LANES, (half + 1) * LANES)
                harm = [yb[j, k, m] for m in range(9)]
                sums = [None] * 9
                for ct in range(0, CHAN // 8, 2):
                    df, dvals = [], [[], [], []]
                    for n in range(2):
                        chans = slice((ct + n) * 8, (ct + n + 1) * 8)
                        f = feat[at, k, chans, :]
                        cots = [da[m, chans, :] for m in range(9)]
                        for l, (low, high) in enumerate(DEGREES):
                            r = g[at, k, l * CHAN + (ct + n) * 8 : l * CHAN + (ct + n + 1) * 8, :]
                            value = r * f if second else r
                            dval = None
                            for m in range(low, high):
                                part = cots[m] * value
                                sums[m] = part if sums[m] is None else sums[m] + part
                                part = cots[m] * harm[m]
                                dval = part if dval is None else dval + part
                            dvals[l].append(dval * f)
                            if second:
                                df_l = dval * r
                                if l == 0:
                                    df.append(df_l)
                                else:
                                    df[n] = df[n] + df_l
                    for l in range(3):
                        rows = slice(l * CHAN + ct * 8, l * CHAN + ct * 8 + 16)
                        dr[h % 2, rows, lanes] = jnp.concatenate(dvals[l], axis=0).astype(BF16)
                    if second:
                        chans = slice(ct * 8, ct * 8 + 16)
                        dfe[chans, k * LANES : (k + 1) * LANES] = jnp.concatenate(df, axis=0).astype(BF16)
                for m in range(9):
                    prt[m * 96 + k * 8 : m * 96 + k * 8 + 8, :] = sums[m]
            lanes = slice(h * 256, (h + 1) * 256)
            dhid = dot(radial_refs[layer][...], dr[h % 2])
            dpr[:, lanes] = (dhid * ds[at, :, lanes]).astype(BF16)
        for h in range(NEIGH // 2):
            lanes = slice(h * 256, (h + 1) * 256)
            drb = dot(winp[layer], dpr[:, lanes])[0:8] * rbd[j, :, lanes]
            q[h * 16 : h * 16 + 8, :] = drb[:, 0:LANES]
            q[h * 16 + 8 : h * 16 + 16, :] = drb[:, LANES:]

    def eight(ref, base):
        total = ref[pl.ds(base, 12, stride=8), :]
        for r in range(1, 8):
            total = total + ref[pl.ds(base + r, 12, stride=8), :]
        return total

    def geometry_back(j):
        x, y, z, env, alive = (geo[j, n] for n in range(5))
        s = x * x + y * y + z * z
        d = [eight(prt, m * 96) for m in range(9)]
        harm = [
            None,
            ROOT3 * x,
            ROOT3 * y,
            ROOT3 * z,
            ROOT15 * x * y,
            ROOT15 * y * z,
            0.5 * ROOT5 * (3.0 * z * z - s),
            ROOT15 * x * z,
            0.5 * ROOT15 * (x * x - y * y),
        ]
        denv = d[0]
        for m in range(1, 9):
            denv = denv + d[m] * harm[m]
        dsq = eight(q, 0) - 2.0 * denv * alive
        d = [None] + [env * value for value in d[1:]]
        d6 = ROOT5 * d[6]
        dx = 2.0 * x * dsq + ROOT3 * d[1] + ROOT15 * (y * d[4] + z * d[7] + x * d[8]) - x * d6
        dy = 2.0 * y * dsq + ROOT3 * d[2] + ROOT15 * (x * d[4] + z * d[5] - y * d[8]) - y * d6
        dz = 2.0 * z * dsq + ROOT3 * d[3] + ROOT15 * (y * d[5] + x * d[7]) + 2.0 * z * d6
        return dx, dy, dz

    radial_refs = (r1_ref, r2_ref)
    mix_refs = (m1_ref, m2_ref)

    def arrive(far):
        for n, d in enumerate(DIRS):
            if (d[0] == 0) == far:
                copy = copies[n]
                copy.wait_recv()

    arrive(False)
    for c in (8, CELLS):
        pg[c * 8 : c * 8 + 8, 0:LANES] = jnp.zeros((8, LANES), F32)
        prt[c * 24 : c * 24 + 24, :] = jnp.zeros((24, LANES), F32)
    tables(9, CELLS, (8, CELLS + 1))

    @pl.loop(0, BLOCKS)
    def _(i):
        j = lax.rem(i + FAR_BLOCKS, BLOCKS)

        @pl.when(i == BLOCKS - FAR_BLOCKS)
        def _():
            arrive(True)
            tables(0, 10, (0, 10))

        centres(j)

        @pl.when(j == 0)
        def _():
            cpos[0] = tiles[OWN, 0:8, :]

        geometry(j)
        for h in range(PAIRS // 256):
            out = dot(embt[...], spoh[j, :, h * 256 : (h + 1) * 256])
            feat[j, 2 * h] = out[:, 0:LANES]
            feat[j, 2 * h + 1] = out[:, LANES:]
        radial(0, j, j)
        gather_sum(j, j, False)
        pre = dot(mix[0], inv[...].astype(BF16))
        sig = sigmoid(pre)
        value = pre * sig
        dnode[j] = sig + value * (1.0 - sig)
        hot = (spec16 == cpos[j, 3:4, :]).astype(BF16)
        state = value + dot(embt[...], hot)
        node[j] = state
        upd[:, pl.ds(pl.multiple_of(j * LANES, LANES), LANES)] = dot(cut[...], state.astype(BF16)).astype(BF16)

    for k in range(NEIGH):
        lanes = slice(k * LANES, (k + 1) * LANES)
        ident = tcell[0, k : k + 1, :] * LANES + slot[0, k : k + 1, :]
        for j in range(BLOCKS):
            oh_site[j * LANES : (j + 1) * LANES, lanes] = (column[j] == ident).astype(BF16)

    radial(1, 0, BLOCKS)
    for h in range(PAIRS // 256):
        out = dot(upd[...], oh_site[:, h * 256 : (h + 1) * 256])
        feat[BLOCKS, 2 * h] = out[:, 0:LANES]
        feat[BLOCKS, 2 * h + 1] = out[:, LANES:]
    gather_sum(0, BLOCKS, True)
    live = (cpos[0, 3:4, :] > -0.5).astype(F32)
    pre = dot(mix[1], inv[...].astype(BF16))
    sig = sigmoid(pre)
    value = pre * sig
    energy = jnp.sum(rocol[0] * node[0] + rocol[1] * value, axis=0, keepdims=True)
    out_ref[3, 0, 0] = live * energy

    sums_back(1, BLOCKS, rocol[1] * live * (sig + value * (1.0 - sig)))
    pair_back(1, 0, BLOCKS, True)
    for m, value in enumerate(geometry_back(0)):
        gacc[0, m] = value
    gacc[1:] = jnp.zeros((BLOCKS - 1, 3, NEIGH, LANES), F32)
    for h in range(BLOCKS // 2):
        rows = slice(h * 256, (h + 1) * 256)
        dupd[:, rows] = dot_nt(dfe[...], oh_site[rows, :]).astype(BF16)
    for j in range(BLOCKS):
        back = dot(cu_ref[...], dupd[:, j * LANES : (j + 1) * LANES])
        if j == 0:
            back = back + rocol[0] * live
        node[j] = back

    returns = []
    for n, (f, dy, dz) in enumerate(DIRS):
        returns.append(
            pltpu.make_async_remote_copy(
                src_ref=gsend.at[cell_number(f, dy, dz)],
                dst_ref=grecv.at[cell_number(f, -dy, -dz)],
                send_sem=send_d.at[n],
                recv_sem=recv_d.at[n],
                device_id=device(f, dy, dz),
                device_id_type=MESH,
            )
        )

    def depart(far):
        @pl.loop(0 if far else 9, 9 if far else CELLS)
        def _(c):
            rows = sc[pl.ds(pl.multiple_of(c * 8, 8), 8), :]
            gsend[c] = (rows + pltpu.roll(rows, 4, 0))[0:4]

        for n, d in enumerate(DIRS):
            if (d[0] == 0) == far:
                copy = returns[n]
                copy.start()

    sc[...] = jnp.zeros_like(sc)

    @pl.loop(0, BLOCKS)
    def _(j):
        sums_back(0, j, node[j] * dnode[j])
        pair_back(0, j, j, False)
        parts = []
        for m, value in enumerate(geometry_back(j)):
            value = (value + gacc[j, m]) * 0.2
            whole = jnp.concatenate([value, -jnp.sum(value, axis=0, keepdims=True)], axis=0)
            high = whole.astype(BF16).astype(F32)
            parts.append((high, whole - high))
        for k in range(NEIGH + 1):
            tile = jnp.zeros((8, LANES), F32)
            for m in range(3):
                for n in range(2):
                    tile = jnp.where(row8 == m + 4 * n, parts[m][n][k : k + 1], tile)
            where = jnp.broadcast_to(tcell[j, k : k + 1, :], (8, LANES))
            lanes = slice(k * LANES, (k + 1) * LANES)
            for c in range(0, CELLS + 1, 2):
                pair = [jnp.where(where == float(c + n), tile, 0.0) for n in range(2)]
                ml[c * 8 : c * 8 + 16, lanes] = jnp.concatenate(pair, axis=0).astype(BF16)
        sc[...] += dot_nt(ml[...], oh[j])

        @pl.when(j == FAR_BLOCKS - 1)
        def _():
            depart(True)

    depart(False)
    for copy in copies:
        copy.wait_send()
    for copy in returns:
        copy.wait_recv()
    total = gsend[OWN]
    for d in DIRS:
        total = total + grecv[cell_number(*d)]
    for m in range(3):
        out_ref[m, 0, 0] = total[m : m + 1]
    for copy in returns:
        copy.wait_send()


def body(sizes, positions, species, neighbours, *weights):
    table = jnp.asarray(site_table())
    vmem = pl.BlockSpec(memory_space=pltpu.VMEM)
    n = len(DIRS)
    scratch = [
        pltpu.VMEM((CELLS, 16, LANES), F32),
        pltpu.VMEM((CELLS * 8 + 8, LANES), BF16),
        pltpu.VMEM((CELLS * 24 + 24, LANES), BF16),
        pltpu.VMEM((CELLS, 4, LANES), F32),
        pltpu.VMEM((CELLS, 4, LANES), F32),
        pltpu.VMEM((BLOCKS, 8, LANES), F32),
        pltpu.VMEM((BLOCKS, NEIGH, LANES), F32),
        pltpu.VMEM((BLOCKS, NEIGH, LANES), F32),
        pltpu.VMEM((BLOCKS, 16, LANES), F32),
        pltpu.VMEM((BLOCKS, LANES, PAIRS + LANES), BF16),
        pltpu.VMEM((BLOCKS * LANES, PAIRS), BF16),
        pltpu.VMEM((CELLS * 8 + 8, PAIRS), F32),
        pltpu.VMEM((96, LANES), F32),
        pltpu.VMEM((BLOCKS, LANES, LANES), F32),
        pltpu.VMEM((BLOCKS, 5, NEIGH, LANES), F32),
        pltpu.VMEM((BLOCKS, NEIGH, 9, 8, LANES), F32),
        pltpu.VMEM((BLOCKS, 16, PAIRS), BF16),
        pltpu.VMEM((BLOCKS, 8, PAIRS), F32),
        pltpu.VMEM((BLOCKS, 16, PAIRS), BF16),
        pltpu.VMEM((BLOCKS + 1, NEIGH, 3 * CHAN, LANES), F32),
        pltpu.VMEM((BLOCKS + 1, NEIGH, CHAN, LANES), F32),
        pltpu.VMEM((BLOCKS + 1, RHID, PAIRS), F32),
        pltpu.VMEM((BLOCKS + 1, 9, CHAN, LANES), F32),
        pltpu.VMEM((3 * CHAN, LANES), F32),
        pltpu.VMEM((BLOCKS, CHAN, LANES), F32),
        pltpu.VMEM((BLOCKS, CHAN, LANES), F32),
        pltpu.VMEM((CHAN, BLOCKS * LANES), BF16),
        pltpu.VMEM((CHAN, BLOCKS * LANES), BF16),
        pltpu.VMEM((9, CHAN, LANES), F32),
        pltpu.VMEM((2, 3 * CHAN, 2 * LANES), BF16),
        pltpu.VMEM((CHAN, PAIRS), BF16),
        pltpu.VMEM((BLOCKS, 3, NEIGH, LANES), F32),
        pltpu.VMEM((9 * 96, LANES), F32),
        pltpu.VMEM((96, LANES), F32),
        pltpu.VMEM((CELLS * 8 + 8, PAIRS + LANES), BF16),
        pltpu.VMEM((CELLS * 8 + 8, LANES), F32),
        pltpu.VMEM((RHID, PAIRS), BF16),
        pltpu.VMEM((2, RHID, 16), BF16),
        pltpu.VMEM((2, 3 * CHAN, RHID), BF16),
        pltpu.VMEM((2, CHAN, 3 * CHAN), BF16),
        pltpu.VMEM((CHAN, CHAN), BF16),
        pltpu.VMEM((CHAN, 16), BF16),
        pltpu.VMEM((2, 16, RHID), BF16),
        pltpu.VMEM((2, CHAN, LANES), F32),
    ] + [pltpu.SemaphoreType.DMA((n,))] * 4
    inputs = (positions, species, neighbours, *weights, table)
    scratch = [pltpu.VMEM(v.shape, v.dtype) for v in inputs] + [pltpu.SemaphoreType.DMA((N_INPUTS,))] + scratch
    out = pl.pallas_call(
        functools.partial(kernel, sizes),
        out_shape=jax.ShapeDtypeStruct((4,) + species.shape, F32),
        in_specs=[pl.BlockSpec(memory_space=pl.ANY)] * N_INPUTS,
        out_specs=vmem,
        scratch_shapes=scratch,
        compiler_params=pltpu.CompilerParams(
            collective_id=0, has_side_effects=True, vmem_limit_bytes=56 << 20
        ),
    )(*inputs)
    return out[3], -out[:3]


def solution(mesh):
    sizes = tuple(mesh.shape[axis] for axis in ("gx", "gy", "gz"))
    grid = ("gx", "gy", "gz", None)
    return jax.shard_map(
        functools.partial(body, sizes),
        mesh=mesh,
        in_specs=(P(None, *grid), P(*grid), P(None, *grid)) + (P(),) * 10,
        out_specs=(P(*grid), P(None, *grid)),
        check_vma=False,
    )
```

```python
import functools
import itertools
import math

import jax
import jax.numpy as jnp
import numpy as np
from jax import lax
from jax.experimental import pallas as pl
from jax.experimental.pallas import tpu as pltpu
from jax.sharding import PartitionSpec as P

MESH = pl.DeviceIdType.MESH
F32 = jnp.float32
BF16 = jnp.bfloat16
LANES = 128
CHAN = 128
RHID = 64
NEIGH = 12
CELLS = 27
N_INPUTS = 14
OWN = 13
BLOCKS = 6
FAR_BLOCKS = 5
PAIRS = NEIGH * LANES
ROOT3 = math.sqrt(3.0)
ROOT5 = math.sqrt(5.0)
ROOT15 = math.sqrt(15.0)
SCALE = 1.0 / math.sqrt(NEIGH)
DEGREES = ((0, 1), (1, 4), (4, 9))
DIRS = [d for d in itertools.product(range(3), (-1, 0, 1), range(3)) if d != (1, 0, 1)]
DIRS.sort(key=lambda d: (d[0] > 0 and d[2] > 0, d[0], d[2], -abs(d[1])))


def cell_number(fx, dy, fz):
    return fx * 9 + (dy + 1) * 3 + fz


LATE = [cell_number(*d) for d in DIRS if d[0] == 0 or d[2] == 0]
EARLY = [cell_number(*d) for d in DIRS if d[0] > 0 and d[2] > 0]


def site_table():
    sites = []
    depth = {-1: (3, 4), 0: range(5), 1: (0, 1)}
    for fx, dy, fz in DIRS:
        for tx, ty, tz in itertools.product(depth[fx - 1], depth[dy], depth[fz - 1]):
            late = (fx - 1) * 5 + tx < 2 or (fz - 1) * 5 + tz < 2
            slots = [ax * 25 + ty * 5 + az for ax in (tx, 4 - tx) for az in (tz, 4 - tz)]
            sites.append((late, slots, cell_number(fx, dy, fz)))
    sites.sort(key=lambda s: not s[0])
    near = (BLOCKS - FAR_BLOCKS) * LANES
    sites = sites[:-near] + [None] * (BLOCKS * LANES - LANES - len(sites)) + sites[-near:]
    table = np.zeros((BLOCKS, 8, LANES), np.float32)
    table[:, 0:4] = -1.0
    table[:, 4] = OWN
    table[0, 0:4] = np.arange(LANES)
    for n, site in enumerate(sites):
        if site is not None:
            table[1 + n // LANES, 0:4, n % LANES] = site[1]
            table[1 + n // LANES, 4, n % LANES] = site[2]
    return table


def dot(a, b):
    return jnp.dot(a, b, preferred_element_type=F32)


def dot_nt(a, b):
    return lax.dot_general(a, b, (((1,), (1,)), ((), ())), preferred_element_type=F32)


def sigmoid(v):
    return 0.5 * jnp.tanh(0.5 * v) + 0.5


def padded_t(value):
    rows, columns = value.shape
    if rows < LANES:
        value = jnp.concatenate([value, jnp.zeros((LANES - rows, columns), F32)], axis=0)
    if columns < LANES:
        value = jnp.concatenate([value, jnp.zeros((LANES, LANES - columns), F32)], axis=1)
    return value.T


def kernel(
    sizes,
    *refs,
):
    n = N_INPUTS
    work(sizes, refs[:n], refs[n], refs[n + 1 : 2 * n + 1], refs[2 * n + 1], *refs[2 * n + 2 :])


def work(
    sizes, sources, out_ref, inputs, input_sem,
    tiles, tpos, tnb, gsend, grecv,
    cpos, code, slot, tcell, oh, oh_site, wide_pos, wide_nb, pg, gs, column, geo, yb, rb, rbd, spoh,
    g, feat, ds, a_s, inv, node, dnode, upd, dupd, da, dr, dfe, gacc, prt, q, ml, sc, dpr,
    win, wout, mix, cut, embt, winp, rocol,
    send_a, recv_a, send_d, recv_d,
):
    (pos_ref, spc_ref, nbr_ref, emb_ref, b1_ref, r1_ref, m1_ref, ro1_ref,
     b2_ref, r2_ref, m2_ref, ro2_ref, cu_ref, con_ref) = inputs
    nx, ny, nz = sizes
    gx, gy, gz = lax.axis_index("gx"), lax.axis_index("gy"), lax.axis_index("gz")
    sigma = 1 - 2 * lax.rem(gx, 2)

    half = nz // 2
    turn = 1 - 2 * lax.div(gz, half)

    def device(fx, dy, fz):
        return (
            lax.rem(gx + (fx - 1) * sigma + nx, nx),
            lax.rem(gy + dy + ny, ny),
            lax.rem(gz + (fz - 1) * turn + nz, nz),
        )

    def seen_from(fx, dy, fz):
        other = 1 - 2 * lax.div(device(fx, dy, fz)[2], half)
        return fx * 9 + (1 - dy) * 3 + 1 - other * turn * (fz - 1)

    barrier = pltpu.get_barrier_semaphore()
    for d in DIRS:
        pl.semaphore_signal(barrier, inc=1, device_id=device(*d), device_id_type=MESH)

    fetches = []
    for n in range(N_INPUTS):
        fetch = pltpu.make_async_copy(sources[n], inputs[n], input_sem.at[n])
        fetch.start()
        fetches.append(fetch)
    for fetch in fetches:
        fetch.wait()

    for m in range(3):
        tiles[OWN, m : m + 1, :] = pos_ref[m, 0, 0]
    tiles[OWN, 3:4, :] = spc_ref[0, 0].astype(F32)
    for k in range(NEIGH):
        tiles[OWN, 4 + k : 5 + k, :] = nbr_ref[k, 0, 0].astype(F32)

    for layer, (b_ref, r_ref, m_ref) in enumerate(((b1_ref, r1_ref, m1_ref), (b2_ref, r2_ref, m2_ref))):
        basis = b_ref[...].astype(F32)
        win[layer] = padded_t(basis)[0:RHID, 0:16].astype(BF16)
        winp[layer] = jnp.concatenate([basis, jnp.zeros_like(basis)], axis=0).astype(BF16)
        for l in range(3):
            block = r_ref[:, l * CHAN : (l + 1) * CHAN].astype(F32)
            wout[layer, l * CHAN : (l + 1) * CHAN, :] = padded_t(block)[:, 0:RHID].astype(BF16)
            block = m_ref[l * CHAN : (l + 1) * CHAN, :].astype(F32)
            mix[layer, :, l * CHAN : (l + 1) * CHAN] = block.T.astype(BF16)
    cut[...] = cu_ref[...].astype(F32).T.astype(BF16)
    emb = jnp.concatenate([emb_ref[...], jnp.zeros((3, CHAN), F32)], axis=0)
    emb_hi = emb.astype(BF16).astype(F32)
    both = jnp.concatenate([emb_hi, emb - emb_hi], axis=0)
    embt[...] = padded_t(both)[:, 0:16].astype(BF16)
    for layer, ro_ref in enumerate((ro1_ref, ro2_ref)):
        rocol[layer] = jnp.broadcast_to(ro_ref[...].reshape(1, CHAN), (LANES, CHAN)).T

    wide_pos[...] = jnp.zeros_like(wide_pos)
    wide_nb[...] = jnp.zeros_like(wide_nb)

    pl.semaphore_wait(barrier, len(DIRS))
    copies = []
    for n, d in enumerate(DIRS):
        place = seen_from(*d)
        copy = pltpu.make_async_remote_copy(
            src_ref=tiles.at[OWN],
            dst_ref=tiles.at[place],
            send_sem=send_a.at[n],
            recv_sem=recv_a.at[place],
            device_id=device(*d),
            device_id_type=MESH,
        )
        copy.start()
        copies.append(copy)

    sigma_f = sigma.astype(F32)
    turn_f = turn.astype(F32)
    row8 = lax.broadcasted_iota(jnp.int32, (8, LANES), 0)
    row16 = lax.broadcasted_iota(jnp.int32, (16, LANES), 0)
    rowf = lax.broadcasted_iota(jnp.int32, (LANES, LANES), 0).astype(F32)
    spec16 = jnp.where(row16 < 8, row16, row16 - 8).astype(F32)
    basis_centre = row8.astype(F32) * (1.0 / 7.0)

    def tables(cells):
        for c in cells:
            top = tiles[c, 0:8, :]
            high = top.astype(BF16).astype(F32)
            low = pltpu.roll(top - high, 4, 0)
            wide_pos[c * 8 : c * 8 + 8, :] = jnp.where(row8 < 4, high, low)
            entries = tiles[c, 4:16, :]
            codes = jnp.floor((entries + 0.5) * (1.0 / LANES))
            wide_nb[c * 24 : c * 24 + 24, :] = jnp.concatenate([codes, entries - LANES * codes], axis=0)
        tpos[...] = wide_pos[...].astype(BF16)
        tnb[...] = wide_nb[...].astype(BF16)

    for j in range(BLOCKS):
        rows = con_ref[j]
        first = jnp.where(turn_f > 0, rows[0:1], rows[1:2])
        own_slot = jnp.where(sigma_f > 0, first, jnp.where(turn_f > 0, rows[2:3], rows[3:4]))
        oh[j, :, PAIRS:] = (rowf == own_slot).astype(BF16)
        ident = jnp.where(own_slot < 0, -1.0, rows[4:5] * LANES + own_slot)
        column[j] = jnp.broadcast_to(ident, (LANES, LANES)).T

    def centres(j):
        rows = con_ref[j]
        cell = jnp.broadcast_to(rows[4:5], (8, LANES))
        hot = oh[j, :, PAIRS:]
        pg[:, 0:LANES] = dot(tpos[...], hot)
        prt[0 : CELLS * 24 + 24, :] = dot(tnb[...], hot)
        acc = [jnp.zeros((8, LANES), F32) for _ in range(4)]
        for c in range(CELLS):
            here = cell == float(c)
            acc[0] = jnp.where(here, pg[c * 8 : c * 8 + 8, 0:LANES], acc[0])
            for part in range(3):
                rows_at = c * 24 + part * 8
                acc[1 + part] = jnp.where(here, prt[rows_at : rows_at + 8, :], acc[1 + part])
        both = jnp.concatenate(acc[1:], axis=0)
        cpos[j] = acc[0] + pltpu.roll(acc[0], 4, 0)
        code[j] = both[0:12]
        slot[j] = both[12:24]

    def geometry(j):
        rows = con_ref[j]
        codes, slots = code[j], slot[j]
        nine = jnp.floor((codes + 0.5) * (1.0 / 9.0))
        three = jnp.floor((codes + 0.5) * (1.0 / 3.0))
        step_x = nine - 1.0
        step_y = three - 3.0 * nine - 1.0
        step_z = codes - 3.0 * three - 1.0
        target = rows[4:5] + 9.0 * sigma_f * step_x + 3.0 * step_y + turn_f * step_z
        tcell[j, 0:12] = target
        tcell[j, 12:13] = rows[4:5]
        for k in range(NEIGH):
            oh[j, :, k * LANES : (k + 1) * LANES] = (rowf == slots[k : k + 1]).astype(BF16)
        for h in range(PAIRS // 256):
            lanes = slice(h * 256, (h + 1) * 256)
            pg[:, lanes] = dot(tpos[...], oh[j, :, lanes])
        for k in range(NEIGH):
            lanes = slice(k * LANES, (k + 1) * LANES)
            here = jnp.broadcast_to(target[k : k + 1], (8, LANES))
            acc = jnp.zeros((8, LANES), F32)
            for c in range(CELLS):
                acc = jnp.where(here == float(c), pg[c * 8 : c * 8 + 8, lanes], acc)
            gs[k * 8 : (k + 1) * 8, :] = acc + pltpu.roll(acc, 4, 0)
        centre = cpos[j]
        x = (gs[pl.ds(0, 12, stride=8), :] + 10.0 * step_x - centre[0:1]) / 5.0
        y = (gs[pl.ds(1, 12, stride=8), :] + 10.0 * step_y - centre[1:2]) / 5.0
        z = (gs[pl.ds(2, 12, stride=8), :] + 10.0 * step_z - centre[2:3]) / 5.0
        species = gs[pl.ds(3, 12, stride=8), :]
        s = x * x + y * y + z * z
        inside = jnp.maximum(1.0 - s, 0.0)
        alive = inside * (species > -0.5).astype(F32)
        env = inside * alive
        geo[j, 0] = x
        geo[j, 1] = y
        geo[j, 2] = z
        geo[j, 3] = env
        geo[j, 4] = alive
        harm = [
            env,
            env * (ROOT3 * x),
            env * (ROOT3 * y),
            env * (ROOT3 * z),
            env * (ROOT15 * x * y),
            env * (ROOT15 * y * z),
            env * (0.5 * ROOT5 * (3.0 * z * z - s)),
            env * (ROOT15 * x * z),
            env * (0.5 * ROOT15 * (x * x - y * y)),
        ]
        for k in range(NEIGH):
            lanes = slice(k * LANES, (k + 1) * LANES)
            for m in range(9):
                yb[j, k, m] = jnp.broadcast_to(harm[m][k : k + 1], (8, LANES))
            t = (jnp.broadcast_to(s[k : k + 1], (8, LANES)) - basis_centre) * 7.0
            e = jnp.exp(-(t * t))
            rb[j, :, lanes] = jnp.concatenate([e, e], axis=0).astype(BF16)
            rbd[j, :, lanes] = e * (-14.0 * t)
            spoh[j, :, lanes] = (spec16 == species[k : k + 1]).astype(BF16)

    def radial(layer, j, at):
        for h in range(PAIRS // 256):
            lanes = slice(h * 256, (h + 1) * 256)
            pre = dot(win[layer], rb[j, :, lanes])
            sig = sigmoid(pre)
            hid = pre * sig
            ds[at, :, lanes] = sig + hid * (1.0 - sig)
            out = dot(wout[layer], hid.astype(BF16))
            g[at, 2 * h] = out[:, 0:LANES]
            g[at, 2 * h + 1] = out[:, LANES:]

    def gather_sum(j, at, second):
        for ct in range(CHAN // 16):
            starts = [ct * 16 + 8 * n for n in range(2)]
            acc = [[None] * 9 for _ in range(2)]
            for k in range(NEIGH):
                harm = [yb[j, k, m] for m in range(9)]
                for n in range(2):
                    f = feat[at, k, pl.ds(starts[n], 8), :]
                    for l, (low, high) in enumerate(DEGREES):
                        here = pl.ds(l * CHAN + starts[n], 8)
                        value = g[at, k, here, :] * f
                        if not second:
                            g[at, k, here, :] = value
                        for m in range(low, high):
                            term = value * harm[m]
                            acc[n][m] = term if k == 0 else acc[n][m] + term
            for n in range(2):
                sums = [a * SCALE for a in acc[n]]
                for m in range(9):
                    a_s[at, m, pl.ds(starts[n], 8), :] = sums[m]
                one = sums[1] * sums[1] + sums[2] * sums[2] + sums[3] * sums[3]
                two = sums[4] * sums[4] + sums[5] * sums[5] + sums[6] * sums[6]
                two = two + sums[7] * sums[7] + sums[8] * sums[8]
                for l, value in enumerate((sums[0], one, two)):
                    inv[pl.ds(l * CHAN + starts[n], 8), :] = value

    def sums_back(layer, at, dpre):
        dinv = dot(mix_refs[layer][...], dpre.astype(BF16))
        da[0] = SCALE * dinv[0:CHAN]
        for l, (low, high) in enumerate(DEGREES[1:], 1):
            part = (2.0 * SCALE) * dinv[l * CHAN : (l + 1) * CHAN]
            for m in range(low, high):
                da[m] = a_s[at, m] * part

    def pair_back(layer, j, at, second):
        for h in range(NEIGH // 2):
            for half in range(2):
                k = 2 * h + half
                lanes = slice(half * LANES, (half + 1) * LANES)
                harm = [yb[j, k, m] for m in range(9)]
                sums = [None] * 9
                for ct in range(0, CHAN // 8, 2):
                    df, dvals = [], [[], [], []]
                    for n in range(2):
                        chans = slice((ct + n) * 8, (ct + n + 1) * 8)
                        f = feat[at, k, chans, :]
                        cots = [da[m, chans, :] for m in range(9)]
                        for l, (low, high) in enumerate(DEGREES):
                            r = g[at, k, l * CHAN + (ct + n) * 8 : l * CHAN + (ct + n + 1) * 8, :]
                            value = r * f if second else r
                            dval = None
                            for m in range(low, high):
                                part = cots[m] * value
                                sums[m] = part if sums[m] is None else sums[m] + part
                                part = cots[m] * harm[m]
                                dval = part if dval is None else dval + part
                            dvals[l].append(dval * f)
                            if second:
                                df_l = dval * r
                                if l == 0:
                                    df.append(df_l)
                                else:
                                    df[n] = df[n] + df_l
                    for l in range(3):
                        rows = slice(l * CHAN + ct * 8, l * CHAN + ct * 8 + 16)
                        dr[h % 2, rows, lanes] = jnp.concatenate(dvals[l], axis=0).astype(BF16)
                    if second:
                        chans = slice(ct * 8, ct * 8 + 16)
                        dfe[chans, k * LANES : (k + 1) * LANES] = jnp.concatenate(df, axis=0).astype(BF16)
                for m in range(9):
                    prt[m * 96 + k * 8 : m * 96 + k * 8 + 8, :] = sums[m]
            lanes = slice(h * 256, (h + 1) * 256)
            dhid = dot(radial_refs[layer][...], dr[h % 2])
            dpr[:, lanes] = (dhid * ds[at, :, lanes]).astype(BF16)
        for h in range(NEIGH // 2):
            lanes = slice(h * 256, (h + 1) * 256)
            drb = dot(winp[layer], dpr[:, lanes])[0:8] * rbd[j, :, lanes]
            q[h * 16 : h * 16 + 8, :] = drb[:, 0:LANES]
            q[h * 16 + 8 : h * 16 + 16, :] = drb[:, LANES:]

    def eight(ref, base):
        total = ref[pl.ds(base, 12, stride=8), :]
        for r in range(1, 8):
            total = total + ref[pl.ds(base + r, 12, stride=8), :]
        return total

    def geometry_back(j):
        x, y, z, env, alive = (geo[j, n] for n in range(5))
        s = x * x + y * y + z * z
        d = [eight(prt, m * 96) for m in range(9)]
        harm = [
            None,
            ROOT3 * x,
            ROOT3 * y,
            ROOT3 * z,
            ROOT15 * x * y,
            ROOT15 * y * z,
            0.5 * ROOT5 * (3.0 * z * z - s),
            ROOT15 * x * z,
            0.5 * ROOT15 * (x * x - y * y),
        ]
        denv = d[0]
        for m in range(1, 9):
            denv = denv + d[m] * harm[m]
        dsq = eight(q, 0) - 2.0 * denv * alive
        d = [None] + [env * value for value in d[1:]]
        d6 = ROOT5 * d[6]
        dx = 2.0 * x * dsq + ROOT3 * d[1] + ROOT15 * (y * d[4] + z * d[7] + x * d[8]) - x * d6
        dy = 2.0 * y * dsq + ROOT3 * d[2] + ROOT15 * (x * d[4] + z * d[5] - y * d[8]) - y * d6
        dz = 2.0 * z * dsq + ROOT3 * d[3] + ROOT15 * (y * d[5] + x * d[7]) + 2.0 * z * d6
        return dx, dy, dz

    radial_refs = (r1_ref, r2_ref)
    mix_refs = (m1_ref, m2_ref)

    def arrive(cells):
        for c in cells:
            copy = pltpu.make_async_copy(tiles.at[c], tiles.at[c], recv_a.at[c])
            copy.wait()

    arrive(EARLY)
    tables(EARLY + [OWN])

    @pl.loop(0, BLOCKS)
    def _(i):
        j = lax.rem(i + FAR_BLOCKS, BLOCKS)

        @pl.when(i == BLOCKS - FAR_BLOCKS)
        def _():
            arrive(LATE)
            tables(LATE)

        centres(j)

        @pl.when(j == 0)
        def _():
            cpos[0] = tiles[OWN, 0:8, :]

        geometry(j)
        for h in range(PAIRS // 256):
            out = dot(embt[...], spoh[j, :, h * 256 : (h + 1) * 256])
            feat[j, 2 * h] = out[:, 0:LANES]
            feat[j, 2 * h + 1] = out[:, LANES:]
        radial(0, j, j)
        gather_sum(j, j, False)
        pre = dot(mix[0], inv[...].astype(BF16))
        sig = sigmoid(pre)
        value = pre * sig
        dnode[j] = sig + value * (1.0 - sig)
        hot = (spec16 == cpos[j, 3:4, :]).astype(BF16)
        state = value + dot(embt[...], hot)
        node[j] = state
        upd[:, pl.ds(pl.multiple_of(j * LANES, LANES), LANES)] = dot(cut[...], state.astype(BF16)).astype(BF16)

    for k in range(NEIGH):
        lanes = slice(k * LANES, (k + 1) * LANES)
        ident = tcell[0, k : k + 1, :] * LANES + slot[0, k : k + 1, :]
        for j in range(BLOCKS):
            oh_site[j * LANES : (j + 1) * LANES, lanes] = (column[j] == ident).astype(BF16)

    radial(1, 0, BLOCKS)
    for h in range(PAIRS // 256):
        out = dot(upd[...], oh_site[:, h * 256 : (h + 1) * 256])
        feat[BLOCKS, 2 * h] = out[:, 0:LANES]
        feat[BLOCKS, 2 * h + 1] = out[:, LANES:]
    gather_sum(0, BLOCKS, True)
    live = (cpos[0, 3:4, :] > -0.5).astype(F32)
    pre = dot(mix[1], inv[...].astype(BF16))
    sig = sigmoid(pre)
    value = pre * sig
    energy = jnp.sum(rocol[0] * node[0] + rocol[1] * value, axis=0, keepdims=True)
    out_ref[3, 0, 0] = live * energy

    sums_back(1, BLOCKS, rocol[1] * live * (sig + value * (1.0 - sig)))
    pair_back(1, 0, BLOCKS, True)
    for m, value in enumerate(geometry_back(0)):
        gacc[0, m] = value
    gacc[1:] = jnp.zeros((BLOCKS - 1, 3, NEIGH, LANES), F32)
    for h in range(BLOCKS // 2):
        rows = slice(h * 256, (h + 1) * 256)
        dupd[:, rows] = dot_nt(dfe[...], oh_site[rows, :]).astype(BF16)
    for j in range(BLOCKS):
        back = dot(cu_ref[...], dupd[:, j * LANES : (j + 1) * LANES])
        if j == 0:
            back = back + rocol[0] * live
        node[j] = back

    returns = []
    for n, d in enumerate(DIRS):
        place = seen_from(*d)
        returns.append(
            pltpu.make_async_remote_copy(
                src_ref=gsend.at[cell_number(*d)],
                dst_ref=grecv.at[place],
                send_sem=send_d.at[n],
                recv_sem=recv_d.at[place],
                device_id=device(*d),
                device_id_type=MESH,
            )
        )

    def depart(cells):
        for c in cells:
            rows = sc[c * 8 : c * 8 + 8, :]
            gsend[c] = (rows + pltpu.roll(rows, 4, 0))[0:4]
        for n, d in enumerate(DIRS):
            if cell_number(*d) in cells:
                copy = returns[n]
                copy.start()

    sc[...] = jnp.zeros_like(sc)

    @pl.loop(0, BLOCKS)
    def _(j):
        sums_back(0, j, node[j] * dnode[j])
        pair_back(0, j, j, False)
        parts = []
        for m, value in enumerate(geometry_back(j)):
            value = (value + gacc[j, m]) * 0.2
            whole = jnp.concatenate([value, -jnp.sum(value, axis=0, keepdims=True)], axis=0)
            high = whole.astype(BF16).astype(F32)
            parts.append((high, whole - high))
        for k in range(NEIGH + 1):
            tile = jnp.zeros((8, LANES), F32)
            for m in range(3):
                for n in range(2):
                    tile = jnp.where(row8 == m + 4 * n, parts[m][n][k : k + 1], tile)
            where = jnp.broadcast_to(tcell[j, k : k + 1, :], (8, LANES))
            lanes = slice(k * LANES, (k + 1) * LANES)
            for c in range(0, CELLS + 1, 2):
                pair = [jnp.where(where == float(c + n), tile, 0.0) for n in range(2)]
                ml[c * 8 : c * 8 + 16, lanes] = jnp.concatenate(pair, axis=0).astype(BF16)
        sc[...] += dot_nt(ml[...], oh[j])

        @pl.when(j == FAR_BLOCKS - 1)
        def _():
            depart(LATE)

    depart(EARLY + [OWN])
    for copy in copies:
        copy.wait_send()
    for c in EARLY + LATE:
        copy = pltpu.make_async_copy(grecv.at[c], grecv.at[c], recv_d.at[c])
        copy.wait()
    total = gsend[OWN]
    for d in DIRS:
        total = total + grecv[cell_number(*d)]
    for m in range(3):
        out_ref[m, 0, 0] = total[m : m + 1]
    for copy in returns:
        copy.wait_send()


def body(sizes, positions, species, neighbours, *weights):
    table = jnp.asarray(site_table())
    vmem = pl.BlockSpec(memory_space=pltpu.VMEM)
    n = len(DIRS)
    scratch = [
        pltpu.VMEM((CELLS, 16, LANES), F32),
        pltpu.VMEM((CELLS * 8 + 8, LANES), BF16),
        pltpu.VMEM((CELLS * 24 + 24, LANES), BF16),
        pltpu.VMEM((CELLS, 4, LANES), F32),
        pltpu.VMEM((CELLS, 4, LANES), F32),
        pltpu.VMEM((BLOCKS, 8, LANES), F32),
        pltpu.VMEM((BLOCKS, NEIGH, LANES), F32),
        pltpu.VMEM((BLOCKS, NEIGH, LANES), F32),
        pltpu.VMEM((BLOCKS, 16, LANES), F32),
        pltpu.VMEM((BLOCKS, LANES, PAIRS + LANES), BF16),
        pltpu.VMEM((BLOCKS * LANES, PAIRS), BF16),
        pltpu.VMEM((CELLS * 8 + 8, LANES), F32),
        pltpu.VMEM((CELLS * 24 + 24, LANES), F32),
        pltpu.VMEM((CELLS * 8 + 8, PAIRS), F32),
        pltpu.VMEM((96, LANES), F32),
        pltpu.VMEM((BLOCKS, LANES, LANES), F32),
        pltpu.VMEM((BLOCKS, 5, NEIGH, LANES), F32),
        pltpu.VMEM((BLOCKS, NEIGH, 9, 8, LANES), F32),
        pltpu.VMEM((BLOCKS, 16, PAIRS), BF16),
        pltpu.VMEM((BLOCKS, 8, PAIRS), F32),
        pltpu.VMEM((BLOCKS, 16, PAIRS), BF16),
        pltpu.VMEM((BLOCKS + 1, NEIGH, 3 * CHAN, LANES), F32),
        pltpu.VMEM((BLOCKS + 1, NEIGH, CHAN, LANES), F32),
        pltpu.VMEM((BLOCKS + 1, RHID, PAIRS), F32),
        pltpu.VMEM((BLOCKS + 1, 9, CHAN, LANES), F32),
        pltpu.VMEM((3 * CHAN, LANES), F32),
        pltpu.VMEM((BLOCKS, CHAN, LANES), F32),
        pltpu.VMEM((BLOCKS, CHAN, LANES), F32),
        pltpu.VMEM((CHAN, BLOCKS * LANES), BF16),
        pltpu.VMEM((CHAN, BLOCKS * LANES), BF16),
        pltpu.VMEM((9, CHAN, LANES), F32),
        pltpu.VMEM((2, 3 * CHAN, 2 * LANES), BF16),
        pltpu.VMEM((CHAN, PAIRS), BF16),
        pltpu.VMEM((BLOCKS, 3, NEIGH, LANES), F32),
        pltpu.VMEM((9 * 96, LANES), F32),
        pltpu.VMEM((96, LANES), F32),
        pltpu.VMEM((CELLS * 8 + 8, PAIRS + LANES), BF16),
        pltpu.VMEM((CELLS * 8 + 8, LANES), F32),
        pltpu.VMEM((RHID, PAIRS), BF16),
        pltpu.VMEM((2, RHID, 16), BF16),
        pltpu.VMEM((2, 3 * CHAN, RHID), BF16),
        pltpu.VMEM((2, CHAN, 3 * CHAN), BF16),
        pltpu.VMEM((CHAN, CHAN), BF16),
        pltpu.VMEM((CHAN, 16), BF16),
        pltpu.VMEM((2, 16, RHID), BF16),
        pltpu.VMEM((2, CHAN, LANES), F32),
    ] + [pltpu.SemaphoreType.DMA((n,)), pltpu.SemaphoreType.DMA((CELLS,))] * 2
    inputs = (positions, species, neighbours, *weights, table)
    scratch = [pltpu.VMEM(v.shape, v.dtype) for v in inputs] + [pltpu.SemaphoreType.DMA((N_INPUTS,))] + scratch
    out = pl.pallas_call(
        functools.partial(kernel, sizes),
        out_shape=jax.ShapeDtypeStruct((4,) + species.shape, F32),
        in_specs=[pl.BlockSpec(memory_space=pl.ANY)] * N_INPUTS,
        out_specs=vmem,
        scratch_shapes=scratch,
        compiler_params=pltpu.CompilerParams(
            collective_id=0, has_side_effects=True, vmem_limit_bytes=56 << 20
        ),
    )(*inputs)
    return out[3], -out[:3]


def solution(mesh):
    sizes = tuple(mesh.shape[axis] for axis in ("gx", "gy", "gz"))
    grid = ("gx", "gy", "gz", None)
    return jax.shard_map(
        functools.partial(body, sizes),
        mesh=mesh,
        in_specs=(P(None, *grid), P(*grid), P(None, *grid)) + (P(),) * 10,
        out_specs=(P(*grid), P(None, *grid)),
        check_vma=False,
    )
```

```python
import functools
import itertools
import math

import jax
import jax.numpy as jnp
import numpy as np
from jax import lax
from jax.experimental import pallas as pl
from jax.experimental.pallas import tpu as pltpu
from jax.sharding import PartitionSpec as P

MESH = pl.DeviceIdType.MESH
F32 = jnp.float32
BF16 = jnp.bfloat16
LANES = 128
CHAN = 128
RHID = 64
NEIGH = 12
CELLS = 27
N_INPUTS = 14
OWN = 13
BLOCKS = 6
FAR_BLOCKS = 5
PAIRS = NEIGH * LANES
ROOT3 = math.sqrt(3.0)
ROOT5 = math.sqrt(5.0)
ROOT15 = math.sqrt(15.0)
SCALE = 1.0 / math.sqrt(NEIGH)
DEGREES = ((0, 1), (1, 4), (4, 9))
DIRS = [d for d in itertools.product(range(3), (-1, 0, 1), range(3)) if d != (1, 0, 1)]
DIRS.sort(key=lambda d: (d[0] > 0 and d[2] > 0, d[0], d[2], -abs(d[1])))


def cell_number(fx, dy, fz):
    return fx * 9 + (dy + 1) * 3 + fz


LATE = [cell_number(*d) for d in DIRS if d[0] == 0 or d[2] == 0]
EARLY = [cell_number(*d) for d in DIRS if d[0] > 0 and d[2] > 0]


def site_table():
    sites = []
    depth = {-1: (3, 4), 0: range(5), 1: (0, 1)}
    for fx, dy, fz in DIRS:
        for tx, ty, tz in itertools.product(depth[fx - 1], depth[dy], depth[fz - 1]):
            late = (fx - 1) * 5 + tx < 2 or (fz - 1) * 5 + tz < 2
            slots = [ax * 25 + ty * 5 + az for ax in (tx, 4 - tx) for az in (tz, 4 - tz)]
            sites.append((late, slots, cell_number(fx, dy, fz)))
    sites.sort(key=lambda s: not s[0])
    near = (BLOCKS - FAR_BLOCKS) * LANES
    sites = sites[:-near] + [None] * (BLOCKS * LANES - LANES - len(sites)) + sites[-near:]
    table = np.zeros((BLOCKS, 8, LANES), np.float32)
    table[:, 0:4] = -1.0
    table[:, 4] = OWN
    table[0, 0:4] = np.arange(LANES)
    for n, site in enumerate(sites):
        if site is not None:
            table[1 + n // LANES, 0:4, n % LANES] = site[1]
            table[1 + n // LANES, 4, n % LANES] = site[2]
    return table


def dot(a, b):
    return jnp.dot(a, b, preferred_element_type=F32)


def dot_nt(a, b):
    return lax.dot_general(a, b, (((1,), (1,)), ((), ())), preferred_element_type=F32)


def sigmoid(v):
    return 0.5 * jnp.tanh(0.5 * v) + 0.5


def padded_t(value):
    rows, columns = value.shape
    if rows < LANES:
        value = jnp.concatenate([value, jnp.zeros((LANES - rows, columns), F32)], axis=0)
    if columns < LANES:
        value = jnp.concatenate([value, jnp.zeros((LANES, LANES - columns), F32)], axis=1)
    return value.T


def kernel(
    sizes,
    *refs,
):
    n = N_INPUTS
    work(sizes, refs[:n], refs[n], refs[n + 1 : 2 * n + 1], refs[2 * n + 1], *refs[2 * n + 2 :])


def work(
    sizes, sources, out_ref, inputs, input_sem,
    tiles, tpos, tnb, gsend, grecv,
    cpos, code, slot, tcell, oh, oh_site, wide_pos, wide_nb, pg, gs, column, geo, yb, rb, rbd, spoh,
    g, feat, ds, a_s, inv, node, dnode, upd, dupd, da, dr, dfe, gacc, prt, q, ml, sc, dpr,
    win, wout, mix, cut, embt, winp, rocol,
    send_a, recv_a, send_d, recv_d,
):
    (pos_ref, spc_ref, nbr_ref, emb_ref, b1_ref, r1_ref, m1_ref, ro1_ref,
     b2_ref, r2_ref, m2_ref, ro2_ref, cu_ref, con_ref) = inputs
    nx, ny, nz = sizes
    gx, gy, gz = lax.axis_index("gx"), lax.axis_index("gy"), lax.axis_index("gz")
    sigma = 1 - 2 * lax.rem(gx, 2)

    half = nz // 2
    turn = 1 - 2 * lax.div(gz, half)

    def device(fx, dy, fz):
        return (
            lax.rem(gx + (fx - 1) * sigma + nx, nx),
            lax.rem(gy + dy + ny, ny),
            lax.rem(gz + (fz - 1) * turn + nz, nz),
        )

    def seen_from(fx, dy, fz):
        other = 1 - 2 * lax.div(device(fx, dy, fz)[2], half)
        return fx * 9 + (1 - dy) * 3 + 1 - other * turn * (fz - 1)

    barrier = pltpu.get_barrier_semaphore()
    for d in DIRS:
        pl.semaphore_signal(barrier, inc=1, device_id=device(*d), device_id_type=MESH)

    fetches = []
    for n in range(N_INPUTS):
        fetch = pltpu.make_async_copy(sources[n], inputs[n], input_sem.at[n])
        fetch.start()
        fetches.append(fetch)
    for fetch in fetches:
        fetch.wait()

    for m in range(3):
        tiles[OWN, 0, m : m + 1, :] = pos_ref[m, 0, 0]
    tiles[OWN, 0, 3:4, :] = spc_ref[0, 0].astype(F32)
    tiles[OWN, 2] = jnp.zeros((4, LANES), F32)
    for n in range(NEIGH // 2):
        word = nbr_ref[n, 0, 0].astype(F32) + 4096.0 * nbr_ref[n + NEIGH // 2, 0, 0].astype(F32)
        tiles[OWN, 1 + n // 4, n % 4 : n % 4 + 1, :] = word

    for layer, (b_ref, r_ref, m_ref) in enumerate(((b1_ref, r1_ref, m1_ref), (b2_ref, r2_ref, m2_ref))):
        basis = b_ref[...].astype(F32)
        win[layer] = padded_t(basis)[0:RHID, 0:16].astype(BF16)
        winp[layer] = jnp.concatenate([basis, jnp.zeros_like(basis)], axis=0).astype(BF16)
        for l in range(3):
            block = r_ref[:, l * CHAN : (l + 1) * CHAN].astype(F32)
            wout[layer, l * CHAN : (l + 1) * CHAN, :] = padded_t(block)[:, 0:RHID].astype(BF16)
            block = m_ref[l * CHAN : (l + 1) * CHAN, :].astype(F32)
            mix[layer, :, l * CHAN : (l + 1) * CHAN] = block.T.astype(BF16)
    cut[...] = cu_ref[...].astype(F32).T.astype(BF16)
    emb = jnp.concatenate([emb_ref[...], jnp.zeros((3, CHAN), F32)], axis=0)
    emb_hi = emb.astype(BF16).astype(F32)
    both = jnp.concatenate([emb_hi, emb - emb_hi], axis=0)
    embt[...] = padded_t(both)[:, 0:16].astype(BF16)
    for layer, ro_ref in enumerate((ro1_ref, ro2_ref)):
        rocol[layer] = jnp.broadcast_to(ro_ref[...].reshape(1, CHAN), (LANES, CHAN)).T

    wide_pos[...] = jnp.zeros_like(wide_pos)
    wide_nb[...] = jnp.zeros_like(wide_nb)

    pl.semaphore_wait(barrier, len(DIRS))
    copies = []
    for n, d in enumerate(DIRS):
        place = seen_from(*d)
        copy = pltpu.make_async_remote_copy(
            src_ref=tiles.at[OWN],
            dst_ref=tiles.at[place],
            send_sem=send_a.at[n],
            recv_sem=recv_a.at[place],
            device_id=device(*d),
            device_id_type=MESH,
        )
        copy.start()
        copies.append(copy)

    sigma_f = sigma.astype(F32)
    turn_f = turn.astype(F32)
    row8 = lax.broadcasted_iota(jnp.int32, (8, LANES), 0)
    row16 = lax.broadcasted_iota(jnp.int32, (16, LANES), 0)
    rowf = lax.broadcasted_iota(jnp.int32, (LANES, LANES), 0).astype(F32)
    spec16 = jnp.where(row16 < 8, row16, row16 - 8).astype(F32)
    basis_centre = row8.astype(F32) * (1.0 / 7.0)

    def tables(cells):
        for c in cells:
            top = tiles[c, 0]
            high = top.astype(BF16).astype(F32)
            wide_pos[c * 8 : c * 8 + 8, :] = jnp.concatenate([high, top - high], axis=0)
            words = jnp.concatenate([tiles[c, 1], tiles[c, 2, 0:2, :]], axis=0)
            later = jnp.floor(words * (1.0 / 4096.0))
            entries = jnp.concatenate([words - 4096.0 * later, later], axis=0)
            codes = jnp.floor(entries * (1.0 / LANES))
            wide_nb[c * 24 : c * 24 + 24, :] = jnp.concatenate([codes, entries - LANES * codes], axis=0)
        tpos[...] = wide_pos[...].astype(BF16)
        tnb[...] = wide_nb[...].astype(BF16)

    for j in range(BLOCKS):
        rows = con_ref[j]
        first = jnp.where(turn_f > 0, rows[0:1], rows[1:2])
        own_slot = jnp.where(sigma_f > 0, first, jnp.where(turn_f > 0, rows[2:3], rows[3:4]))
        oh[j, :, PAIRS:] = (rowf == own_slot).astype(BF16)
        ident = jnp.where(own_slot < 0, -1.0, rows[4:5] * LANES + own_slot)
        column[j] = jnp.broadcast_to(ident, (LANES, LANES)).T

    def centres(j):
        rows = con_ref[j]
        cell = jnp.broadcast_to(rows[4:5], (8, LANES))
        hot = oh[j, :, PAIRS:]
        pg[:, 0:LANES] = dot(tpos[...], hot)
        prt[0 : CELLS * 24 + 24, :] = dot(tnb[...], hot)
        acc = [jnp.zeros((8, LANES), F32) for _ in range(4)]
        for c in range(CELLS):
            here = cell == float(c)
            acc[0] = jnp.where(here, pg[c * 8 : c * 8 + 8, 0:LANES], acc[0])
            for part in range(3):
                rows_at = c * 24 + part * 8
                acc[1 + part] = jnp.where(here, prt[rows_at : rows_at + 8, :], acc[1 + part])
        both = jnp.concatenate(acc[1:], axis=0)
        cpos[j] = acc[0] + pltpu.roll(acc[0], 4, 0)
        code[j] = both[0:12]
        slot[j] = both[12:24]

    def geometry(j):
        rows = con_ref[j]
        codes, slots = code[j], slot[j]
        nine = jnp.floor((codes + 0.5) * (1.0 / 9.0))
        three = jnp.floor((codes + 0.5) * (1.0 / 3.0))
        step_x = nine - 1.0
        step_y = three - 3.0 * nine - 1.0
        step_z = codes - 3.0 * three - 1.0
        target = rows[4:5] + 9.0 * sigma_f * step_x + 3.0 * step_y + turn_f * step_z
        tcell[j, 0:12] = target
        tcell[j, 12:13] = rows[4:5]
        for k in range(NEIGH):
            oh[j, :, k * LANES : (k + 1) * LANES] = (rowf == slots[k : k + 1]).astype(BF16)
        for h in range(PAIRS // 256):
            lanes = slice(h * 256, (h + 1) * 256)
            pg[:, lanes] = dot(tpos[...], oh[j, :, lanes])
        for k in range(NEIGH):
            lanes = slice(k * LANES, (k + 1) * LANES)
            here = jnp.broadcast_to(target[k : k + 1], (8, LANES))
            acc = jnp.zeros((8, LANES), F32)
            for c in range(CELLS):
                acc = jnp.where(here == float(c), pg[c * 8 : c * 8 + 8, lanes], acc)
            gs[k * 8 : (k + 1) * 8, :] = acc + pltpu.roll(acc, 4, 0)
        centre = cpos[j]
        x = (gs[pl.ds(0, 12, stride=8), :] + 10.0 * step_x - centre[0:1]) / 5.0
        y = (gs[pl.ds(1, 12, stride=8), :] + 10.0 * step_y - centre[1:2]) / 5.0
        z = (gs[pl.ds(2, 12, stride=8), :] + 10.0 * step_z - centre[2:3]) / 5.0
        species = gs[pl.ds(3, 12, stride=8), :]
        s = x * x + y * y + z * z
        inside = jnp.maximum(1.0 - s, 0.0)
        alive = inside * (species > -0.5).astype(F32)
        env = inside * alive
        geo[j, 0] = x
        geo[j, 1] = y
        geo[j, 2] = z
        geo[j, 3] = env
        geo[j, 4] = alive
        harm = [
            env,
            env * (ROOT3 * x),
            env * (ROOT3 * y),
            env * (ROOT3 * z),
            env * (ROOT15 * x * y),
            env * (ROOT15 * y * z),
            env * (0.5 * ROOT5 * (3.0 * z * z - s)),
            env * (ROOT15 * x * z),
            env * (0.5 * ROOT15 * (x * x - y * y)),
        ]
        for k in range(NEIGH):
            lanes = slice(k * LANES, (k + 1) * LANES)
            for m in range(9):
                yb[j, k, m] = jnp.broadcast_to(harm[m][k : k + 1], (8, LANES))
            t = (jnp.broadcast_to(s[k : k + 1], (8, LANES)) - basis_centre) * 7.0
            e = jnp.exp(-(t * t))
            rb[j, :, lanes] = jnp.concatenate([e, e], axis=0).astype(BF16)
            rbd[j, :, lanes] = e * (-14.0 * t)
            spoh[j, :, lanes] = (spec16 == species[k : k + 1]).astype(BF16)

    def radial(layer, j, at):
        for h in range(PAIRS // 256):
            lanes = slice(h * 256, (h + 1) * 256)
            pre = dot(win[layer], rb[j, :, lanes])
            sig = sigmoid(pre)
            hid = pre * sig
            ds[at, :, lanes] = sig + hid * (1.0 - sig)
            out = dot(wout[layer], hid.astype(BF16))
            g[at, 2 * h] = out[:, 0:LANES]
            g[at, 2 * h + 1] = out[:, LANES:]

    def gather_sum(j, at, second):
        for ct in range(CHAN // 16):
            starts = [ct * 16 + 8 * n for n in range(2)]
            acc = [[None] * 9 for _ in range(2)]
            for k in range(NEIGH):
                harm = [yb[j, k, m] for m in range(9)]
                for n in range(2):
                    f = feat[at, k, pl.ds(starts[n], 8), :]
                    for l, (low, high) in enumerate(DEGREES):
                        here = pl.ds(l * CHAN + starts[n], 8)
                        value = g[at, k, here, :] * f
                        if not second:
                            g[at, k, here, :] = value
                        for m in range(low, high):
                            term = value * harm[m]
                            acc[n][m] = term if k == 0 else acc[n][m] + term
            for n in range(2):
                sums = [a * SCALE for a in acc[n]]
                for m in range(9):
                    a_s[at, m, pl.ds(starts[n], 8), :] = sums[m]
                one = sums[1] * sums[1] + sums[2] * sums[2] + sums[3] * sums[3]
                two = sums[4] * sums[4] + sums[5] * sums[5] + sums[6] * sums[6]
                two = two + sums[7] * sums[7] + sums[8] * sums[8]
                for l, value in enumerate((sums[0], one, two)):
                    inv[pl.ds(l * CHAN + starts[n], 8), :] = value

    def sums_back(layer, at, dpre):
        dinv = dot(mix_refs[layer][...], dpre.astype(BF16))
        da[0] = SCALE * dinv[0:CHAN]
        for l, (low, high) in enumerate(DEGREES[1:], 1):
            part = (2.0 * SCALE) * dinv[l * CHAN : (l + 1) * CHAN]
            for m in range(low, high):
                da[m] = a_s[at, m] * part

    def pair_back(layer, j, at, second):
        for h in range(NEIGH // 2):
            for half in range(2):
                k = 2 * h + half
                lanes = slice(half * LANES, (half + 1) * LANES)
                harm = [yb[j, k, m] for m in range(9)]
                sums = [None] * 9
                for ct in range(0, CHAN // 8, 2):
                    df, dvals = [], [[], [], []]
                    for n in range(2):
                        chans = slice((ct + n) * 8, (ct + n + 1) * 8)
                        f = feat[at, k, chans, :]
                        cots = [da[m, chans, :] for m in range(9)]
                        for l, (low, high) in enumerate(DEGREES):
                            r = g[at, k, l * CHAN + (ct + n) * 8 : l * CHAN + (ct + n + 1) * 8, :]
                            value = r * f if second else r
                            dval = None
                            for m in range(low, high):
                                part = cots[m] * value
                                sums[m] = part if sums[m] is None else sums[m] + part
                                part = cots[m] * harm[m]
                                dval = part if dval is None else dval + part
                            dvals[l].append(dval * f)
                            if second:
                                df_l = dval * r
                                if l == 0:
                                    df.append(df_l)
                                else:
                                    df[n] = df[n] + df_l
                    for l in range(3):
                        rows = slice(l * CHAN + ct * 8, l * CHAN + ct * 8 + 16)
                        dr[h % 2, rows, lanes] = jnp.concatenate(dvals[l], axis=0).astype(BF16)
                    if second:
                        chans = slice(ct * 8, ct * 8 + 16)
                        dfe[chans, k * LANES : (k + 1) * LANES] = jnp.concatenate(df, axis=0).astype(BF16)
                for m in range(9):
                    prt[m * 96 + k * 8 : m * 96 + k * 8 + 8, :] = sums[m]
            lanes = slice(h * 256, (h + 1) * 256)
            dhid = dot(radial_refs[layer][...], dr[h % 2])
            dpr[:, lanes] = (dhid * ds[at, :, lanes]).astype(BF16)
        for h in range(NEIGH // 2):
            lanes = slice(h * 256, (h + 1) * 256)
            drb = dot(winp[layer], dpr[:, lanes])[0:8] * rbd[j, :, lanes]
            q[h * 16 : h * 16 + 8, :] = drb[:, 0:LANES]
            q[h * 16 + 8 : h * 16 + 16, :] = drb[:, LANES:]

    def eight(ref, base):
        total = ref[pl.ds(base, 12, stride=8), :]
        for r in range(1, 8):
            total = total + ref[pl.ds(base + r, 12, stride=8), :]
        return total

    def geometry_back(j):
        x, y, z, env, alive = (geo[j, n] for n in range(5))
        s = x * x + y * y + z * z
        d = [eight(prt, m * 96) for m in range(9)]
        harm = [
            None,
            ROOT3 * x,
            ROOT3 * y,
            ROOT3 * z,
            ROOT15 * x * y,
            ROOT15 * y * z,
            0.5 * ROOT5 * (3.0 * z * z - s),
            ROOT15 * x * z,
            0.5 * ROOT15 * (x * x - y * y),
        ]
        denv = d[0]
        for m in range(1, 9):
            denv = denv + d[m] * harm[m]
        dsq = eight(q, 0) - 2.0 * denv * alive
        d = [None] + [env * value for value in d[1:]]
        d6 = ROOT5 * d[6]
        dx = 2.0 * x * dsq + ROOT3 * d[1] + ROOT15 * (y * d[4] + z * d[7] + x * d[8]) - x * d6
        dy = 2.0 * y * dsq + ROOT3 * d[2] + ROOT15 * (x * d[4] + z * d[5] - y * d[8]) - y * d6
        dz = 2.0 * z * dsq + ROOT3 * d[3] + ROOT15 * (y * d[5] + x * d[7]) + 2.0 * z * d6
        return dx, dy, dz

    radial_refs = (r1_ref, r2_ref)
    mix_refs = (m1_ref, m2_ref)

    def arrive(cells):
        for c in cells:
            copy = pltpu.make_async_copy(tiles.at[c], tiles.at[c], recv_a.at[c])
            copy.wait()

    arrive(EARLY)
    tables(EARLY + [OWN])

    @pl.loop(0, BLOCKS)
    def _(i):
        j = lax.rem(i + FAR_BLOCKS, BLOCKS)

        @pl.when(i == BLOCKS - FAR_BLOCKS)
        def _():
            arrive(LATE)
            tables(LATE)

        centres(j)

        @pl.when(j == 0)
        def _():
            cpos[0, 0:4, :] = tiles[OWN, 0]

        geometry(j)
        for h in range(PAIRS // 256):
            out = dot(embt[...], spoh[j, :, h * 256 : (h + 1) * 256])
            feat[j, 2 * h] = out[:, 0:LANES]
            feat[j, 2 * h + 1] = out[:, LANES:]
        radial(0, j, j)
        gather_sum(j, j, False)
        pre = dot(mix[0], inv[...].astype(BF16))
        sig = sigmoid(pre)
        value = pre * sig
        dnode[j] = sig + value * (1.0 - sig)
        hot = (spec16 == cpos[j, 3:4, :]).astype(BF16)
        state = value + dot(embt[...], hot)
        node[j] = state
        upd[:, pl.ds(pl.multiple_of(j * LANES, LANES), LANES)] = dot(cut[...], state.astype(BF16)).astype(BF16)

    for k in range(NEIGH):
        lanes = slice(k * LANES, (k + 1) * LANES)
        ident = tcell[0, k : k + 1, :] * LANES + slot[0, k : k + 1, :]
        for j in range(BLOCKS):
            oh_site[j * LANES : (j + 1) * LANES, lanes] = (column[j] == ident).astype(BF16)

    radial(1, 0, BLOCKS)
    for h in range(PAIRS // 256):
        out = dot(upd[...], oh_site[:, h * 256 : (h + 1) * 256])
        feat[BLOCKS, 2 * h] = out[:, 0:LANES]
        feat[BLOCKS, 2 * h + 1] = out[:, LANES:]
    gather_sum(0, BLOCKS, True)
    live = (cpos[0, 3:4, :] > -0.5).astype(F32)
    pre = dot(mix[1], inv[...].astype(BF16))
    sig = sigmoid(pre)
    value = pre * sig
    energy = jnp.sum(rocol[0] * node[0] + rocol[1] * value, axis=0, keepdims=True)
    out_ref[3, 0, 0] = live * energy

    sums_back(1, BLOCKS, rocol[1] * live * (sig + value * (1.0 - sig)))
    pair_back(1, 0, BLOCKS, True)
    for m, value in enumerate(geometry_back(0)):
        gacc[0, m] = value
    gacc[1:] = jnp.zeros((BLOCKS - 1, 3, NEIGH, LANES), F32)
    for h in range(BLOCKS // 2):
        rows = slice(h * 256, (h + 1) * 256)
        dupd[:, rows] = dot_nt(dfe[...], oh_site[rows, :]).astype(BF16)
    for j in range(BLOCKS):
        back = dot(cu_ref[...], dupd[:, j * LANES : (j + 1) * LANES])
        if j == 0:
            back = back + rocol[0] * live
        node[j] = back

    returns = []
    for n, d in enumerate(DIRS):
        place = seen_from(*d)
        returns.append(
            pltpu.make_async_remote_copy(
                src_ref=gsend.at[cell_number(*d)],
                dst_ref=grecv.at[place],
                send_sem=send_d.at[n],
                recv_sem=recv_d.at[place],
                device_id=device(*d),
                device_id_type=MESH,
            )
        )

    def depart(cells):
        for c in cells:
            rows = sc[c * 8 : c * 8 + 8, :]
            gsend[c] = (rows + pltpu.roll(rows, 4, 0))[0:4]
        for n, d in enumerate(DIRS):
            if cell_number(*d) in cells:
                copy = returns[n]
                copy.start()

    sc[...] = jnp.zeros_like(sc)

    @pl.loop(0, BLOCKS)
    def _(j):
        sums_back(0, j, node[j] * dnode[j])
        pair_back(0, j, j, False)
        parts = []
        for m, value in enumerate(geometry_back(j)):
            value = (value + gacc[j, m]) * 0.2
            whole = jnp.concatenate([value, -jnp.sum(value, axis=0, keepdims=True)], axis=0)
            high = whole.astype(BF16).astype(F32)
            parts.append((high, whole - high))
        for k in range(NEIGH + 1):
            tile = jnp.zeros((8, LANES), F32)
            for m in range(3):
                for n in range(2):
                    tile = jnp.where(row8 == m + 4 * n, parts[m][n][k : k + 1], tile)
            where = jnp.broadcast_to(tcell[j, k : k + 1, :], (8, LANES))
            lanes = slice(k * LANES, (k + 1) * LANES)
            for c in range(0, CELLS + 1, 2):
                pair = [jnp.where(where == float(c + n), tile, 0.0) for n in range(2)]
                ml[c * 8 : c * 8 + 16, lanes] = jnp.concatenate(pair, axis=0).astype(BF16)
        sc[...] += dot_nt(ml[...], oh[j])

        @pl.when(j == FAR_BLOCKS - 1)
        def _():
            depart(LATE)

    depart(EARLY + [OWN])
    for copy in copies:
        copy.wait_send()
    for c in EARLY + LATE:
        copy = pltpu.make_async_copy(grecv.at[c], grecv.at[c], recv_d.at[c])
        copy.wait()
    total = gsend[OWN]
    for d in DIRS:
        total = total + grecv[cell_number(*d)]
    for m in range(3):
        out_ref[m, 0, 0] = total[m : m + 1]
    for copy in returns:
        copy.wait_send()


def body(sizes, positions, species, neighbours, *weights):
    table = jnp.asarray(site_table())
    vmem = pl.BlockSpec(memory_space=pltpu.VMEM)
    n = len(DIRS)
    scratch = [
        pltpu.VMEM((CELLS, 3, 4, LANES), F32),
        pltpu.VMEM((CELLS * 8 + 8, LANES), BF16),
        pltpu.VMEM((CELLS * 24 + 24, LANES), BF16),
        pltpu.VMEM((CELLS, 4, LANES), F32),
        pltpu.VMEM((CELLS, 4, LANES), F32),
        pltpu.VMEM((BLOCKS, 8, LANES), F32),
        pltpu.VMEM((BLOCKS, NEIGH, LANES), F32),
        pltpu.VMEM((BLOCKS, NEIGH, LANES), F32),
        pltpu.VMEM((BLOCKS, 16, LANES), F32),
        pltpu.VMEM((BLOCKS, LANES, PAIRS + LANES), BF16),
        pltpu.VMEM((BLOCKS * LANES, PAIRS), BF16),
        pltpu.VMEM((CELLS * 8 + 8, LANES), F32),
        pltpu.VMEM((CELLS * 24 + 24, LANES), F32),
        pltpu.VMEM((CELLS * 8 + 8, PAIRS), F32),
        pltpu.VMEM((96, LANES), F32),
        pltpu.VMEM((BLOCKS, LANES, LANES), F32),
        pltpu.VMEM((BLOCKS, 5, NEIGH, LANES), F32),
        pltpu.VMEM((BLOCKS, NEIGH, 9, 8, LANES), F32),
        pltpu.VMEM((BLOCKS, 16, PAIRS), BF16),
        pltpu.VMEM((BLOCKS, 8, PAIRS), F32),
        pltpu.VMEM((BLOCKS, 16, PAIRS), BF16),
        pltpu.VMEM((BLOCKS + 1, NEIGH, 3 * CHAN, LANES), F32),
        pltpu.VMEM((BLOCKS + 1, NEIGH, CHAN, LANES), F32),
        pltpu.VMEM((BLOCKS + 1, RHID, PAIRS), F32),
        pltpu.VMEM((BLOCKS + 1, 9, CHAN, LANES), F32),
        pltpu.VMEM((3 * CHAN, LANES), F32),
        pltpu.VMEM((BLOCKS, CHAN, LANES), F32),
        pltpu.VMEM((BLOCKS, CHAN, LANES), F32),
        pltpu.VMEM((CHAN, BLOCKS * LANES), BF16),
        pltpu.VMEM((CHAN, BLOCKS * LANES), BF16),
        pltpu.VMEM((9, CHAN, LANES), F32),
        pltpu.VMEM((2, 3 * CHAN, 2 * LANES), BF16),
        pltpu.VMEM((CHAN, PAIRS), BF16),
        pltpu.VMEM((BLOCKS, 3, NEIGH, LANES), F32),
        pltpu.VMEM((9 * 96, LANES), F32),
        pltpu.VMEM((96, LANES), F32),
        pltpu.VMEM((CELLS * 8 + 8, PAIRS + LANES), BF16),
        pltpu.VMEM((CELLS * 8 + 8, LANES), F32),
        pltpu.VMEM((RHID, PAIRS), BF16),
        pltpu.VMEM((2, RHID, 16), BF16),
        pltpu.VMEM((2, 3 * CHAN, RHID), BF16),
        pltpu.VMEM((2, CHAN, 3 * CHAN), BF16),
        pltpu.VMEM((CHAN, CHAN), BF16),
        pltpu.VMEM((CHAN, 16), BF16),
        pltpu.VMEM((2, 16, RHID), BF16),
        pltpu.VMEM((2, CHAN, LANES), F32),
    ] + [pltpu.SemaphoreType.DMA((n,)), pltpu.SemaphoreType.DMA((CELLS,))] * 2
    inputs = (positions, species, neighbours, *weights, table)
    scratch = [pltpu.VMEM(v.shape, v.dtype) for v in inputs] + [pltpu.SemaphoreType.DMA((N_INPUTS,))] + scratch
    out = pl.pallas_call(
        functools.partial(kernel, sizes),
        out_shape=jax.ShapeDtypeStruct((4,) + species.shape, F32),
        in_specs=[pl.BlockSpec(memory_space=pl.ANY)] * N_INPUTS,
        out_specs=vmem,
        scratch_shapes=scratch,
        compiler_params=pltpu.CompilerParams(
            collective_id=0, has_side_effects=True, vmem_limit_bytes=56 << 20
        ),
    )(*inputs)
    return out[3], -out[:3]


def solution(mesh):
    sizes = tuple(mesh.shape[axis] for axis in ("gx", "gy", "gz"))
    grid = ("gx", "gy", "gz", None)
    return jax.shard_map(
        functools.partial(body, sizes),
        mesh=mesh,
        in_specs=(P(None, *grid), P(*grid), P(None, *grid)) + (P(),) * 10,
        out_specs=(P(*grid), P(None, *grid)),
        check_vma=False,
    )
```
